128 devices in a mesh: dp: 32 (over z_lo, x, y), mp: 4 (over z_hi, core).
Axes of the slice: x: 4, y: 4, z: 4 (z_hi: 2, z_lo: 2; z = z_hi * 2 + z_lo), core: 2. Of those that a mesh axis runs over, the one named last changes fastest.
Arguments:
- tokens: bfloat16 [32768, 8192], P('dp'), may hold values from -500 to 500
- norm_gain: bfloat16 [8192], replicated, may hold values from 0.099609375 to 1.8984375
- query_weight: bfloat16 [8192, 4096], P('dp', 'mp'), may hold values from -0.0625 to 0.0625
- query_bias: bfloat16 [4096], P('mp'), may hold values from -3 to 3
- keyval_weight: bfloat16 [8192, 4, 256], P('dp', 'mp'), may hold values from -0.0625 to 0.0625
- keyval_bias: bfloat16 [4, 256], P('mp'), may hold values from -4 to 4
- visual_keyval: bfloat16 [32, 1024, 4, 256], P('dp', 'mp'), may hold values from -70 to 70
- caption_image: int32 [512], P('dp'), may hold values from 0 to 31, as said below
- caption_length: int32 [512], P('dp'), may hold values from 1 to 64
- image_owner: int32 [32], replicated, may hold values from 0 to 31, each once
Outputs:
- attended: bfloat16 [32768, 4096], P('dp', 'mp')
The draws below stay inside these ranges and needn't reach their ends.
Inputs may be any that keep to these rules, and one draw needn't show every extreme that they name: `caption_image`: Non-decreasing; caption c has image c // 16 or the image before it; image 0 starts at caption 0 and every later image i starts at a caption between i * 16 + 1 and i * 16 + 16 // 2, so every image has between 8 and 24 captions. `image_owner`: each row of visual_keyval holds exactly one image.
All inputs are finite; a program needn't handle non-finite values.
Results may differ from the reference program's by a relative error of at most 0.0049.
The reference program's roundings to bfloat16 on the way count: a program that leaves them out, or rounds other values in their place, can miss the bound.
Values may be sent and summed in bfloat16 or wider, within the bound.
No kernel may reach another device: no remote copies, remote signals or barrier semaphores. Data moves between devices by JAX's collectives and lax.ppermute only.
A program may use at most 192 MiB of HBM per device.

```python
import math
import jax
import jax.numpy as jnp
from jax import lax

D = 8192
HEADS = 32
KVH = 4
HD = 128
VTOK = 1024
LEN = 64
CAP_DEV = 16
CAPTIONS = 512
IMAGES = 32


def draw_tokens(key, part):
    key = jax.random.fold_in(key, 1)
    key_base, key_row, key_col = jax.random.split(key, 3)
    shape = (CAPTIONS * LEN, D)
    base = jnp.clip(jax.random.normal(key_base, shape, jnp.float32), -4.0, 4.0)
    row_scale = jnp.exp(jax.random.uniform(key_row, (shape[0], 1), jnp.float32) * math.log(10.0))
    col_scale = jnp.exp(jax.random.uniform(key_col, (1, D), jnp.float32) * math.log(10.0))
    return (base * row_scale * col_scale).astype(jnp.bfloat16)


def draw_visual_keyval(key, part):
    key = jax.random.fold_in(key, 3)
    shape = (IMAGES, VTOK, KVH, 2 * HD)
    base = jnp.clip(jax.random.normal(key, shape, jnp.float32), -6.0, 6.0)
    return base.astype(jnp.bfloat16)


def draw_caption_image(key, part):
    key = jax.random.fold_in(key, 2)
    half_count = CAP_DEV // 2
    image_ids = jnp.arange(IMAGES, dtype=jnp.int32)
    offsets = jax.random.randint(key, (IMAGES,), 1, half_count + 1, jnp.int32)
    offsets = jnp.where(image_ids == 0, 0, offsets)
    offsets = jnp.where(image_ids == 1, half_count, offsets)
    offsets = jnp.where(image_ids == 2, 1, offsets).astype(jnp.int32)
    starts = (image_ids * CAP_DEV + offsets).astype(jnp.int32)
    caption_ids = jnp.arange(CAPTIONS, dtype=jnp.int32)
    later = (starts[None, 1:] <= caption_ids[:, None]).astype(jnp.int32)
    return jnp.sum(later, axis=1).astype(jnp.int32)


def draw_caption_length(key, part):
    key = jax.random.fold_in(key, 4)
    lengths = jax.random.randint(key, (CAPTIONS,), 1, LEN + 1, jnp.int32)
    return lengths.at[0].set(LEN).at[1].set(1)


def level_of(rng, extent, shards, least, high):
    def one(dim, shards_of):
        draws = jax.random.uniform(jax.random.fold_in(jax.random.fold_in(rng, 6), dim), (shards_of,), jnp.float32, least / len(shards), high / len(shards))
        return jnp.repeat(jnp.exp(draws), extent[dim] // shards_of).reshape((-1,) + (1,) * (len(extent) - dim - 1))

    gain = one(*shards[0])
    for cut in shards[1:]:
        gain = gain * one(*cut)
    return gain


def centred(stream_key, extent, scale, limit, pieces=(), kind=jnp.bfloat16):
    values = scale * jax.random.normal(stream_key, extent, jnp.float32)
    if pieces:
        values = values * level_of(stream_key, extent, pieces, -0.22, 0.18)
    return jnp.clip(values, -limit, limit).astype(kind)


def setup_inputs(seed: int = 0) -> dict:
    splits = jax.random.split(jax.random.key(seed), 11)
    return {
        "tokens": draw_tokens(jax.random.fold_in(splits[10], 71), 0),
        "norm_gain": jnp.clip(1.0 + 0.18 * jax.random.normal(splits[1], (D,), jnp.float32), 0.099609375, 1.8984375).astype(jnp.bfloat16),
        "query_weight": centred(splits[2], (D, HEADS * HD), D ** -0.5, 0.0625, ((0, 32), (1, 4))),
        "query_bias": centred(splits[3], (HEADS * HD,), 0.5, 3.0, ((0, 4),)),
        "keyval_weight": centred(splits[4], (D, KVH, 2 * HD), D ** -0.5, 0.0625, ((0, 32), (1, 4))),
        "keyval_bias": centred(splits[5], (KVH, 2 * HD), 1.0, 4.0, ((0, 4),)),
        "visual_keyval": draw_visual_keyval(jax.random.fold_in(splits[10], 71), 0),
        "caption_image": draw_caption_image(jax.random.fold_in(splits[10], 71), 0),
        "caption_length": draw_caption_length(jax.random.fold_in(splits[10], 71), 0),
        "image_owner": jax.random.permutation(splits[9], IMAGES).astype(jnp.int32),
    }


ROPE_BASE = 1000000.0

def rotate(values_in, positions):
    half_width = values_in.shape[-1] // 2
    freqs = ROPE_BASE ** (-jnp.arange(half_width, dtype=jnp.float32) / half_width)
    angles = positions[:, None] * freqs[None, :]
    target = (positions.shape[0],) + (1,) * (values_in.ndim - 3) + (half_width,)
    cosine = jnp.cos(angles).reshape(target)
    sine_part = jnp.sin(angles).reshape(target)
    first = values_in[..., :half_width]
    second = values_in[..., half_width:]
    return jnp.concatenate([first * cosine - second * sine_part, second * cosine + first * sine_part], -1)

def attend_one(query_rot, key_text, value_text, visual, length_now):
    head_dim = query_rot.shape[-1]
    score_scale = 1.0 / jnp.sqrt(jnp.float32(head_dim))
    query_wide = query_rot.astype(jnp.float32)
    visual_keys = visual[..., :head_dim].astype(jnp.float32)
    visual_vals = visual[..., head_dim:].astype(jnp.float32)
    score_visual = jnp.einsum('tgjd,sgd->gjts', query_wide, visual_keys) * score_scale
    score_text = jnp.einsum('tgjd,ugd->gjtu', query_wide, key_text.astype(jnp.float32)) * score_scale
    slots = jnp.arange(query_rot.shape[0], dtype=jnp.int32)
    causal_mask = slots[None, :] <= slots[:, None]
    score_text = jnp.where(causal_mask, score_text, -jnp.inf)
    top_score = jnp.maximum(lax.optimization_barrier(jnp.max(score_visual, -1)), lax.optimization_barrier(jnp.max(score_text, -1)))[..., None]
    exp_visual = jnp.exp(score_visual - top_score)
    exp_text = jnp.exp(score_text - top_score)
    weight_sum = lax.optimization_barrier(jnp.sum(exp_visual, -1, keepdims=True)) + lax.optimization_barrier(jnp.sum(exp_text, -1, keepdims=True))
    prob_visual = (exp_visual / weight_sum).astype(jnp.bfloat16)
    prob_text = (exp_text / weight_sum).astype(jnp.bfloat16)
    mixed = jnp.einsum('gjts,sgd->tgjd', prob_visual.astype(jnp.float32), visual_vals)
    mixed = mixed + jnp.einsum('gjtu,ugd->tgjd', prob_text.astype(jnp.float32), value_text.astype(jnp.float32))
    valid = slots < length_now
    return jnp.where(valid[:, None, None, None], mixed, 0.0).astype(jnp.bfloat16)

def reference(tokens, norm_gain, query_weight, query_bias, keyval_weight, keyval_bias, visual_keyval, caption_image, caption_length, image_owner):
    widened = tokens.astype(jnp.float32)
    mean_square = lax.optimization_barrier(jnp.mean(widened * widened, -1, keepdims=True))
    normed = (widened * lax.rsqrt(mean_square + 1e-06) * norm_gain.astype(jnp.float32)).astype(jnp.bfloat16)
    query_full = jnp.dot(normed, query_weight, preferred_element_type=jnp.float32) + query_bias.astype(jnp.float32)
    keyval = jnp.dot(normed, keyval_weight.reshape(D, KVH * 2 * HD), preferred_element_type=jnp.float32)
    keyval = keyval + keyval_bias.reshape(-1).astype(jnp.float32)
    group_size = HEADS // KVH
    query_full = query_full.reshape(CAPTIONS, LEN, KVH, group_size, HD)
    keyval = keyval.reshape(CAPTIONS, LEN, KVH, 2 * HD)
    positions = (VTOK + jnp.arange(LEN, dtype=jnp.int32)).astype(jnp.float32)
    query_rot = rotate(query_full, positions).astype(jnp.bfloat16)
    key_text = rotate(keyval[..., :HD], positions).astype(jnp.bfloat16)
    value_text = keyval[..., HD:].astype(jnp.bfloat16)
    owner_of = jnp.take(image_owner, caption_image).astype(jnp.int32)

    def per_caption(items):
        query_now, key_now, value_now, owner_now, length_now = items
        visual = lax.dynamic_index_in_dim(visual_keyval, owner_now, 0, keepdims=False)
        return attend_one(query_now, key_now, value_now, visual, length_now)
    outputs = lax.map(per_caption, (query_rot, key_text, value_text, owner_of, caption_length))
    return outputs.reshape(CAPTIONS * LEN, HEADS * HD)
```

```python
import functools
import math

import jax
import jax.numpy as jnp
from jax import lax
from jax.experimental import pallas as pl
from jax.experimental.pallas import tpu as pltpu
from jax.sharding import Mesh
from jax.sharding import PartitionSpec as P

ROPE_BASE = 1000000.0
UNIT = 128
SET_D = (8, 9)
SET_A = (0, 1)
SET_B = (2, 3, 4)
SET_C = (5, 6, 7)
MESH_AXES = ("zl", "x", "y", "zh", "core")
SIZES = {"zl": 2, "x": 4, "y": 4, "zh": 2, "core": 2}
DP = ("zl", "x", "y")
MP = ("zh", "core")
PLANE = ("x", "y")


def shift(value, axis, by):
    size = SIZES[axis]
    return lax.ppermute(value, axis, [(i, (i + by) % size) for i in range(size)])


def norm_body(tokens_ref, gain_ref, out_ref):
    wide = tokens_ref[...].astype(jnp.float32)
    mean_square = jnp.mean(wide * wide, -1, keepdims=True)
    out_ref[...] = (
        wide * lax.rsqrt(mean_square + 1e-06) * gain_ref[...].astype(jnp.float32)
    ).astype(jnp.bfloat16)


def norm_rows(tokens, gain):
    rows, width = tokens.shape
    tile = 128
    return pl.pallas_call(
        norm_body,
        grid=(rows // tile,),
        in_specs=[
            pl.BlockSpec((tile, width), lambda i: (i, 0)),
            pl.BlockSpec((1, width), lambda i: (0, 0)),
        ],
        out_specs=pl.BlockSpec((tile, width), lambda i: (i, 0)),
        out_shape=jax.ShapeDtypeStruct((rows, width), jnp.bfloat16),
        compiler_params=pltpu.CompilerParams(vmem_limit_bytes=40 * 2**20),
        cost_estimate=pl.CostEstimate(
            flops=4 * rows * width, bytes_accessed=4 * rows * width, transcendentals=rows
        ),
        name="norm_rows",
    )(tokens, gain.reshape(1, width))


def project_body(plan, units, has_acc, last, piece, *refs):
    refs = list(refs)
    index_ref = refs.pop(0)
    x_refs = [refs.pop(0) for _ in range(4)]
    count = 1 + max(a for step in plan for a in step)
    w_refs = [refs.pop(0) for _ in range(count)]
    acc_in = refs.pop(0) if has_acc else None
    if last:
        bias_ref, cos_ref, sin_ref = refs.pop(0), refs.pop(0), refs.pop(0)
    out_ref = refs.pop(0)
    w_buf = refs.pop(0)
    acc = refs.pop(0) if last else out_ref
    step = pl.program_id(0)
    steps = len(plan)
    width = w_buf.shape[1]

    seen = {}
    for s, parts in enumerate(plan):
        seen.setdefault(tuple(parts), []).append(s)
    for parts, where in seen.items():
        lo, hi = min(where), max(where)

        @pl.when((step >= lo) & (step <= hi))
        def _(parts=parts):
            at = 0
            for a in parts:
                rows = w_refs[a].shape[0]
                w_buf[pl.ds(at, rows), :] = w_refs[a][...]
                at += rows

    tile = 256

    def add(first):
        def one(i, carry):
            rows = pl.ds(pl.multiple_of(i * tile, tile), tile)
            x = jnp.concatenate([r[rows, :] for r in x_refs], axis=1)
            part = jnp.dot(x, w_buf[...], preferred_element_type=jnp.float32)
            if first:
                if has_acc:
                    acc[rows, :] = acc_in[rows, :] + part
                else:
                    acc[rows, :] = part
            else:
                acc[rows, :] += part
            return carry

        lax.fori_loop(0, x_refs[0].shape[0] // tile, one, 0)

    @pl.when(step == 0)
    def _():
        add(True)

    if steps > 1:

        @pl.when(step > 0)
        def _():
            add(False)

    if last:

        @pl.when(step == steps - 1)
        def _():
            def rope(i, carry):
                rows = pl.ds(pl.multiple_of(i * 64, 64), 64)
                for j, unit in enumerate(units):
                    cols = slice(j * UNIT, (j + 1) * UNIT)
                    value = acc[rows, cols] + bias_ref[:, cols]
                    if unit != 9:
                        value = value * cos_ref[...] + pltpu.roll(value, 64, 1) * sin_ref[...]
                    out_ref[rows, cols] = value.astype(jnp.bfloat16)
                return carry

            lax.fori_loop(0, out_ref.shape[0] // 64, rope, 0)


def project(normed, index, weights, plan, units, acc=None, tail=None):
    rows = normed.shape[0]
    width = weights[0].shape[1]
    steps = len(plan)
    last = tail is not None
    specs = [
        pl.BlockSpec((rows, 256), functools.partial(lambda j, k, idx: (0, idx[4 * k + j]), j))
        for j in range(4)
    ]
    args = [normed] * 4
    for a, w in enumerate(weights):
        uses = [s for s, parts in enumerate(plan) if a in parts]
        if len(uses) == 1:
            specs.append(pl.BlockSpec(w.shape, lambda k, idx: (0, 0)))
        else:
            lo, hi = min(uses), max(uses)
            assert w.shape[0] == 1024 * len(uses)
            specs.append(
                pl.BlockSpec(
                    (1024, width),
                    functools.partial(lambda lo, hi, k, idx: (jnp.clip(k, lo, hi) - lo, 0), lo, hi),
                )
            )
        args.append(w)
    if acc is not None:
        specs.append(pl.BlockSpec((rows, width), lambda k, idx: (0, 0)))
        args.append(acc)
    scratch = [pltpu.VMEM((1024, width), jnp.bfloat16)]
    if last:
        bias, cos, sin = tail
        specs += [
            pl.BlockSpec((1, width), lambda k, idx: (0, 0)),
            pl.BlockSpec(cos.shape, lambda k, idx: (0, 0)),
            pl.BlockSpec(sin.shape, lambda k, idx: (0, 0)),
        ]
        args += [bias, cos, sin]
        scratch.append(pltpu.VMEM((rows, width), jnp.float32))
    kind = jnp.bfloat16 if last else jnp.float32
    return pl.pallas_call(
        functools.partial(project_body, plan, units, acc is not None, last, None),
        grid_spec=pltpu.PrefetchScalarGridSpec(
            num_scalar_prefetch=1,
            grid=(steps,),
            in_specs=specs,
            out_specs=pl.BlockSpec((rows, width), lambda k, idx: (0, 0)),
            scratch_shapes=scratch,
        ),
        out_shape=jax.ShapeDtypeStruct((rows, width), kind),
        compiler_params=pltpu.CompilerParams(vmem_limit_bytes=52 * 2**20),
        cost_estimate=pl.CostEstimate(
            flops=2 * rows * 1024 * steps * width,
            bytes_accessed=steps * 2 * 1024 * (rows + width) + rows * width * 4,
            transcendentals=0,
        ),
        name="project",
    )(index, *args)


def attend_body(counts, length, which_ref, len_ref, *refs):
    refs = list(refs)
    q_refs = [refs.pop(0) for _ in counts]
    text_ref, visual_ref, out_ref = refs
    now = pl.program_id(0)
    used = len_ref[now]
    head_dim = UNIT
    factor = 1.0 / math.sqrt(head_dim) * math.log2(math.e)
    nt = (((1,), (1,)), ((), ()))

    def run(rows):
        parts = []
        for ref, count in zip(q_refs, counts):
            parts += [ref[0:rows, j * UNIT : (j + 1) * UNIT] for j in range(count)]
        query = jnp.concatenate(parts, axis=0)
        heads = len(parts)
        visual = visual_ref[...].reshape(-1, 2 * head_dim)
        text = text_ref[...]
        sv = lax.dot_general(
            query, visual[:, :head_dim], nt, preferred_element_type=jnp.float32
        )
        st = lax.dot_general(query, text[:, :head_dim], nt, preferred_element_type=jnp.float32)
        at = lax.broadcasted_iota(jnp.int32, st.shape, 0) % rows
        st = jnp.where(lax.broadcasted_iota(jnp.int32, st.shape, 1) <= at, st, -jnp.inf)
        top = jnp.maximum(
            jnp.max(sv, -1, keepdims=True), jnp.max(st, -1, keepdims=True)
        )
        ev = jnp.exp2((sv - top) * factor)
        et = jnp.exp2((st - top) * factor)
        total = jnp.sum(ev, -1, keepdims=True) + jnp.sum(et, -1, keepdims=True)
        inverse = 1.0 / total
        pv = (ev * inverse).astype(jnp.bfloat16)
        pt = (et * inverse).astype(jnp.bfloat16)
        mixed = jnp.dot(pv, visual[:, head_dim:], preferred_element_type=jnp.float32)
        mixed += jnp.dot(pt, text[:, head_dim:], preferred_element_type=jnp.float32)
        keep = lax.broadcasted_iota(jnp.int32, (rows, head_dim), 0) < used
        for h in range(heads):
            out_ref[0:rows, h * UNIT : (h + 1) * UNIT] = jnp.where(
                keep, mixed[h * rows : (h + 1) * rows], 0.0
            ).astype(jnp.bfloat16)
        if rows < length:
            out_ref[rows:length, :] = jnp.zeros((length - rows, out_ref.shape[1]), jnp.bfloat16)

    tiles = length // 16
    for tile in range(1, tiles + 1):

        @pl.when((used > 16 * (tile - 1)) & (used <= 16 * tile))
        def _(tile=tile):
            run(16 * tile)


def attend(which, lengths, queries, text, visual):
    captions = which.shape[0]
    rows = queries[0].shape[0]
    length = rows // captions
    counts = tuple(q.shape[1] // UNIT for q in queries)
    width = sum(counts) * UNIT
    relays, _, chunk, depth = visual.shape
    return pl.pallas_call(
        functools.partial(attend_body, counts, length),
        grid_spec=pltpu.PrefetchScalarGridSpec(
            num_scalar_prefetch=2,
            grid=(captions,),
            in_specs=[
                pl.BlockSpec((length, q.shape[1]), lambda c, which, lens: (c, 0)) for q in queries
            ]
            + [
                pl.BlockSpec((length, text.shape[1]), lambda c, which, lens: (c, 0)),
                pl.BlockSpec(
                    (relays, 1, chunk, depth), lambda c, which, lens: (0, which[c], 0, 0)
                ),
            ],
            out_specs=pl.BlockSpec((length, width), lambda c, which, lens: (c, 0)),
        ),
        out_shape=jax.ShapeDtypeStruct((rows, width), jnp.bfloat16),
        compiler_params=pltpu.CompilerParams(vmem_limit_bytes=52 * 2**20),
        cost_estimate=pl.CostEstimate(
            flops=4 * rows * width * relays * chunk,
            bytes_accessed=4 * rows * width,
            transcendentals=rows * (width // UNIT) * relays * chunk,
        ),
        name="attend",
    )(which, lengths, *queries, text, visual)


def ring_gather(unit, axis):
    half = unit.shape[0] // 2
    before = shift(unit, axis, 1)
    after = shift(unit, axis, -1)
    far_head = shift(before[:half], axis, 1)
    far_tail = shift(after[half:], axis, -1)
    return before, after, far_head, far_tail


def line_gather(piece, axis):
    return jnp.concatenate(
        [piece, shift(piece, axis, 1), shift(piece, axis, -1), shift(piece, axis, 2)], axis=0
    )


def on_device(
    tokens,
    norm_gain,
    query_weight,
    query_bias,
    keyval_weight,
    keyval_bias,
    visual_keyval,
    caption_image,
    caption_length,
    image_owner,
):
    zl, x, y = (lax.axis_index(a) for a in DP)
    here = lax.axis_index(DP)
    rows = tokens.shape[0]
    depth = query_weight.shape[0]
    head_dim = keyval_weight.shape[2] // 2
    weight = jnp.concatenate([query_weight, keyval_weight.reshape(depth, -1)], axis=1)
    bias = jnp.concatenate([query_bias, keyval_bias.reshape(-1)]).astype(jnp.float32)[None]

    def pick(array, units):
        return jnp.concatenate([array[:, u * UNIT : (u + 1) * UNIT] for u in units], axis=1)

    w_d, w_a, w_b, w_c = (pick(weight, s) for s in (SET_D, SET_A, SET_B, SET_C))

    a_other = shift(w_a, "zl", 1)
    d_own = lax.all_gather(w_d, PLANE, axis=0, tiled=True)
    line_b = line_gather(w_b, "y")
    line_c = line_gather(w_c, "x")
    cross_b = shift(line_b, "zl", 1)
    cross_c = shift(line_c, "zl", 1)
    d_cross = shift(d_own, "zl", 1)
    both = jnp.where(zl == 0, jnp.concatenate([w_a, a_other]), jnp.concatenate([a_other, w_a]))
    a_full = lax.all_gather(both, PLANE, axis=0, tiled=True)
    own_b = ring_gather(line_b, "x")
    own_c = ring_gather(line_c, "y")
    far_b = ring_gather(cross_b, "x")
    far_c = ring_gather(cross_c, "y")

    tok_local = visual_keyval.shape[1]
    kv_heads = visual_keyval.shape[2]
    images = image_owner.shape[0]
    chunk = tok_local // images
    spread = visual_keyval.reshape(images, chunk, kv_heads, 2 * head_dim).transpose(0, 2, 1, 3)
    spread = spread.reshape(images * kv_heads, chunk, 2 * head_dim)
    held = lax.all_to_all(spread, DP + MP, split_axis=0, concat_axis=0, tiled=True)
    held = held.reshape(images, kv_heads * chunk, 2 * head_dim)
    target = jnp.arange(images, dtype=jnp.int32)
    wanted = jnp.stack([image_owner[jnp.maximum(target - 1, 0)], image_owner[target]], axis=1)
    selector = (wanted[:, :, None] == target[None, None, :]).astype(jnp.bfloat16)
    sent = jnp.einsum(
        "isn,ntd->istd", selector, held, preferred_element_type=jnp.float32
    ).astype(jnp.bfloat16)
    visual = lax.all_to_all(sent, DP, split_axis=0, concat_axis=0, tiled=True)
    which = jnp.clip(caption_image - here + 1, 0, 1).astype(jnp.int32)

    half = head_dim // 2
    length = rows // caption_image.shape[0]
    vis_tokens = tok_local * kv_heads
    freqs = ROPE_BASE ** (-jnp.arange(half, dtype=jnp.float32) / half)
    positions = (vis_tokens + jnp.arange(length, dtype=jnp.int32)).astype(jnp.float32)
    angles = positions[:, None] * freqs[None, :]
    cos = jnp.concatenate([jnp.cos(angles)] * 2, axis=1)
    sin = jnp.concatenate([-jnp.sin(angles), jnp.sin(angles)], axis=1)

    def tail(units):
        return pick(bias, units), cos, sin

    normed = norm_rows(tokens, norm_gain)
    line = jnp.arange(4, dtype=jnp.int32)
    turn = jnp.array([0, -1, 1, 2], jnp.int32)

    def line_index_b(plane, at_x):
        return plane * 16 + at_x % 4 * 4 + (y + turn) % 4

    def line_index_c(plane, at_y):
        return plane * 16 + (x + turn) % 4 * 4 + at_y % 4

    other = 1 - zl

    def ring_project(units, line_of, at, line_arr, own, cross_arr, cross):
        before, after, head, tail_half = own
        fbefore, fafter, fhead, ftail = cross
        acc = project(
            normed,
            jnp.concatenate([line_of(zl, at), line_of(zl, at - 1), line_of(zl, at + 1)]),
            [line_arr, before, after],
            [(0,), (1,), (2,)],
            units,
        )
        acc = project(
            normed,
            jnp.concatenate(
                [line_of(zl, at + 2), line_of(other, at), line_of(other, at - 1), line_of(other, at + 1)]
            ),
            [head, tail_half, cross_arr, fbefore, fafter],
            [(0, 1), (2,), (3,), (4,)],
            units,
            acc,
        )
        return project(
            normed, line_of(other, at + 2), [fhead, ftail], [(0, 1)], units, acc, tail(units)
        )

    span = jnp.arange(16, dtype=jnp.int32)
    acc_d = project(normed, zl * 16 + span, [d_own], [(0,)] * 4, SET_D)
    q_b = ring_project(SET_B, line_index_b, x, line_b, own_b, cross_b, far_b)
    q_c = ring_project(SET_C, line_index_c, y, line_c, own_c, cross_c, far_c)
    text = project(normed, other * 16 + span, [d_cross], [(0,)] * 4, SET_D, acc_d, tail(SET_D))
    order_a = jnp.stack([span, span + 16], axis=1).reshape(-1)
    q_a = project(normed, order_a, [a_full], [(0,)] * 8, SET_A, None, tail(SET_A))
    return attend(which, caption_length, [q_a, q_b, q_c], text, visual)


def solution(mesh):
    grid = Mesh(mesh.devices.reshape(tuple(SIZES[a] for a in MESH_AXES)), MESH_AXES)
    placed = (
        P(DP, None),
        P(),
        P(DP, MP),
        P(MP),
        P(DP, MP, None),
        P(MP, None),
        P(DP, MP, None, None),
        P(DP),
        P(DP),
        P(),
    )
    return jax.shard_map(
        on_device, mesh=grid, in_specs=placed, out_specs=P(DP, MP), check_vma=False
    )
```

```python
import functools
import math

import jax
import jax.numpy as jnp
from jax import lax
from jax.experimental import pallas as pl
from jax.experimental.pallas import tpu as pltpu
from jax.sharding import Mesh
from jax.sharding import PartitionSpec as P

ROPE_BASE = 1000000.0
UNIT = 128
PIECE = 256
STEP = 1024
SET_D = (8, 9)
SET_B = (0, 1, 2, 3)
SET_C = (4, 5, 6, 7)
MESH_AXES = ("zl", "x", "y", "zh", "core")
SIZES = {"zl": 2, "x": 4, "y": 4, "zh": 2, "core": 2}
DP = ("zl", "x", "y")
MP = ("zh", "core")
PLANE = ("x", "y")
MIB = 2**20


def shift(value, axis, by):
    size = SIZES[axis]
    return lax.ppermute(value, axis, [(i, (i + by) % size) for i in range(size)])


def whole():
    return pl.BlockSpec(memory_space=pltpu.VMEM)


def norm_body(tokens_ref, gain_ref, out_ref, buf, sems):
    rows = tokens_ref.shape[0]
    depth, tile = buf.shape[:2]
    count = rows // tile

    def copy(i, slot):
        at = pl.multiple_of(i * tile, tile)
        return pltpu.make_async_copy(tokens_ref.at[pl.ds(at, tile)], buf.at[slot], sems.at[slot])

    for i in range(depth - 1):
        copy(i, i).start()
    gain = gain_ref[...].astype(jnp.float32)

    def one(i, carry):
        slot = lax.rem(i, depth)

        @pl.when(i + depth - 1 < count)
        def _():
            copy(i + depth - 1, lax.rem(i + depth - 1, depth)).start()

        copy(i, slot).wait()
        for part in range(tile // 16):
            wide = buf[slot, part * 16 : (part + 1) * 16, :].astype(jnp.float32)
            mean_square = jnp.mean(wide * wide, -1, keepdims=True)
            out_ref[pl.ds(pl.multiple_of(i * tile + part * 16, 16), 16), :] = (
                wide * lax.rsqrt(mean_square + 1e-06) * gain
            ).astype(jnp.bfloat16)
        return carry

    lax.fori_loop(0, count, one, 0)


def norm_rows(tokens, gain):
    rows, width = tokens.shape
    depth, tile = 4, 64
    return pl.pallas_call(
        norm_body,
        in_specs=[pl.BlockSpec(memory_space=pl.ANY), whole()],
        out_specs=whole(),
        out_shape=jax.ShapeDtypeStruct((rows, width), jnp.bfloat16),
        scratch_shapes=[
            pltpu.VMEM((depth, tile, width), jnp.bfloat16),
            pltpu.SemaphoreType.DMA((depth,)),
        ],
        compiler_params=pltpu.CompilerParams(vmem_limit_bytes=24 * MIB),
        cost_estimate=pl.CostEstimate(
            flops=4 * rows * width, bytes_accessed=4 * rows * width, transcendentals=rows
        ),
        name="norm_rows",
    )(tokens, gain.reshape(1, width))


def project_body(rows_of, has_acc, units, index_ref, x_ref, *refs):
    refs = list(refs)
    w_refs = [refs.pop(0) for _ in rows_of]
    acc_in = refs.pop(0) if has_acc else None
    if units:
        bias_ref, cos_ref, sin_ref = refs.pop(0), refs.pop(0), refs.pop(0)
    out_ref, w_buf, sems = refs.pop(0), refs.pop(0), refs.pop(0)
    acc = refs.pop(0) if units else out_ref
    steps = sum(rows_of) // STEP

    copies = [[] for _ in range(steps)]
    at = 0
    for ref, count in zip(w_refs, rows_of):
        done = 0
        while done < count:
            s, into = divmod(at, STEP)
            size = min(count - done, STEP - into)
            copies[s].append(
                pltpu.make_async_copy(
                    ref.at[pl.ds(done, size)],
                    w_buf.at[pl.ds(at, size)],
                    sems.at[s, len(copies[s])],
                )
            )
            done += size
            at += size
    for group in copies:
        for copy in group:
            copy.start()

    tile = 256
    for s in range(steps):
        for copy in copies[s]:
            copy.wait()
        w = w_buf.at[pl.ds(s * STEP, STEP)]
        cols = [
            pl.ds(pl.multiple_of(index_ref[4 * s + j] * PIECE, PIECE), PIECE) for j in range(4)
        ]
        for m in range(0, x_ref.shape[0], tile):
            x = jnp.concatenate([x_ref[m : m + tile, c] for c in cols], axis=1)
            part = jnp.dot(x, w[...], preferred_element_type=jnp.float32)
            if s > 0:
                part += acc[m : m + tile, :]
            elif has_acc:
                part += acc_in[m : m + tile, :]
            acc[m : m + tile, :] = part

    if units:

        def rope(i, carry):
            rows = pl.ds(pl.multiple_of(i * 64, 64), 64)
            for j, unit in enumerate(units):
                cols = slice(j * UNIT, (j + 1) * UNIT)
                value = acc[rows, cols] + bias_ref[:, cols]
                if unit != 9:
                    value = value * cos_ref[...] + pltpu.roll(value, 64, 1) * sin_ref[...]
                out_ref[rows, cols] = value.astype(jnp.bfloat16)
            return carry

        lax.fori_loop(0, out_ref.shape[0] // 64, rope, 0)


def project(normed, index, weights, acc=None, units=None, tail=()):
    rows = normed.shape[0]
    width = weights[0].shape[1]
    rows_of = [w.shape[0] for w in weights]
    total = sum(rows_of)
    scratch = [
        pltpu.VMEM((total, width), jnp.bfloat16),
        pltpu.SemaphoreType.DMA((total // STEP, 4)),
    ]
    if units:
        scratch.append(pltpu.VMEM((rows, width), jnp.float32))
    accs = [] if acc is None else [acc]
    return pl.pallas_call(
        functools.partial(project_body, rows_of, acc is not None, units),
        in_specs=[pl.BlockSpec(memory_space=pltpu.SMEM), whole()]
        + [pl.BlockSpec(memory_space=pl.ANY)] * len(weights)
        + [whole()] * (len(accs) + len(tail)),
        out_specs=whole(),
        out_shape=jax.ShapeDtypeStruct((rows, width), jnp.bfloat16 if units else jnp.float32),
        scratch_shapes=scratch,
        compiler_params=pltpu.CompilerParams(vmem_limit_bytes=30 * MIB),
        cost_estimate=pl.CostEstimate(
            flops=2 * rows * total * width, bytes_accessed=2 * total * width, transcendentals=0
        ),
        name="project",
    )(index, normed, *weights, *accs, *tail)


def attend_body(length, has_before, which_ref, len_ref, q_ref, text_ref, visual_ref, *refs):
    out_ref = refs[-1]
    now = pl.program_id(0)
    used = len_ref[now]
    heads = q_ref.shape[1] // UNIT
    factor = 1.0 / math.sqrt(UNIT) * math.log2(math.e)
    nt = (((1,), (1,)), ((), ()))

    def run(rows):
        query = jnp.concatenate(
            [q_ref[0:rows, j * UNIT : (j + 1) * UNIT] for j in range(heads)], axis=0
        )
        visual = visual_ref[...].reshape(-1, 2 * UNIT)
        text = text_ref[...]
        sv = lax.dot_general(query, visual[:, :UNIT], nt, preferred_element_type=jnp.float32)
        st = lax.dot_general(query, text[:, :UNIT], nt, preferred_element_type=jnp.float32)
        at = lax.broadcasted_iota(jnp.int32, st.shape, 0) % rows
        st = jnp.where(lax.broadcasted_iota(jnp.int32, st.shape, 1) <= at, st, -jnp.inf)
        top = jnp.maximum(jnp.max(sv, -1, keepdims=True), jnp.max(st, -1, keepdims=True))
        ev = jnp.exp2((sv - top) * factor)
        et = jnp.exp2((st - top) * factor)
        inverse = 1.0 / (jnp.sum(ev, -1, keepdims=True) + jnp.sum(et, -1, keepdims=True))
        pv = (ev * inverse).astype(jnp.bfloat16)
        pt = (et * inverse).astype(jnp.bfloat16)
        mixed = jnp.dot(pv, visual[:, UNIT:], preferred_element_type=jnp.float32)
        mixed += jnp.dot(pt, text[:, UNIT:], preferred_element_type=jnp.float32)
        keep = lax.broadcasted_iota(jnp.int32, (rows, UNIT), 0) < used
        for h in range(heads):
            out_ref[0:rows, h * UNIT : (h + 1) * UNIT] = jnp.where(
                keep, mixed[h * rows : (h + 1) * rows], 0.0
            ).astype(jnp.bfloat16)
        if rows < length:
            out_ref[rows:length, :] = jnp.zeros((length - rows, out_ref.shape[1]), jnp.bfloat16)

    for tile in range(1, length // 16 + 1):

        @pl.when((used > 16 * (tile - 1)) & (used <= 16 * tile))
        def _(tile=tile):
            run(16 * tile)


def attend(which, lengths, query, text, visual, place, out_width, before=None):
    captions = which.shape[0]
    rows, width = query.shape
    length = rows // captions
    relays, _, chunk, depth = visual.shape
    befores = [] if before is None else [before]
    return pl.pallas_call(
        functools.partial(attend_body, length, before is not None),
        grid_spec=pltpu.PrefetchScalarGridSpec(
            num_scalar_prefetch=2,
            grid=(captions,),
            in_specs=[
                pl.BlockSpec((length, width), lambda c, which, lens: (c, 0)),
                pl.BlockSpec((length, text.shape[1]), lambda c, which, lens: (c, 0)),
                pl.BlockSpec(
                    (relays, 1, chunk, depth), lambda c, which, lens: (0, which[c], 0, 0)
                ),
            ]
            + [pl.BlockSpec(memory_space=pl.ANY)] * len(befores),
            out_specs=pl.BlockSpec((length, width), lambda c, which, lens: (c, place)),
        ),
        out_shape=jax.ShapeDtypeStruct((rows, out_width), jnp.bfloat16),
        input_output_aliases={5: 0} if befores else {},
        compiler_params=pltpu.CompilerParams(vmem_limit_bytes=24 * MIB),
        cost_estimate=pl.CostEstimate(
            flops=4 * rows * width * relays * chunk,
            bytes_accessed=4 * rows * width,
            transcendentals=rows * (width // UNIT) * relays * chunk,
        ),
        name="attend",
    )(which, lengths, query, text, visual, *befores)


def line_gather(piece, axis):
    return jnp.concatenate(
        [piece, shift(piece, axis, 1), shift(piece, axis, -1), shift(piece, axis, 2)], axis=0
    )


def on_device(
    tokens,
    norm_gain,
    query_weight,
    query_bias,
    keyval_weight,
    keyval_bias,
    visual_keyval,
    caption_image,
    caption_length,
    image_owner,
):
    zl, x, y = (lax.axis_index(a) for a in DP)
    here = lax.axis_index(DP)
    rows = tokens.shape[0]
    depth = query_weight.shape[0]
    head_dim = keyval_weight.shape[2] // 2
    weight = jnp.concatenate([query_weight, keyval_weight.reshape(depth, -1)], axis=1)
    bias = jnp.concatenate([query_bias, keyval_bias.reshape(-1)]).astype(jnp.float32)[None]

    def pick(array, units):
        return array[:, units[0] * UNIT : (units[-1] + 1) * UNIT]

    w_d, w_b, w_c = (pick(weight, s) for s in (SET_D, SET_B, SET_C))

    d_own = lax.all_gather(w_d, PLANE, axis=0, tiled=True)
    line_b = line_gather(w_b, "y")
    line_c = line_gather(w_c, "x")
    cross_b = shift(line_b, "zl", 1)
    cross_c = shift(line_c, "zl", 1)
    d_cross = shift(d_own, "zl", 1)

    def big(line, cross, axis):
        own_before, own_after = shift(line, axis, 1), shift(line, axis, -1)
        own_far = shift(own_before, axis, 1)
        cross_before, cross_after = shift(cross, axis, 1), shift(cross, axis, -1)
        cross_far = shift(cross_after, axis, -1)
        return [line, own_before, own_after], [own_far, cross, cross_before, cross_after], cross_far

    parts_b = big(line_b, cross_b, "x")
    parts_c = big(line_c, cross_c, "y")

    tok_local = visual_keyval.shape[1]
    kv_heads = visual_keyval.shape[2]
    images = image_owner.shape[0]
    chunk = tok_local // images
    spread = visual_keyval.reshape(images, chunk, kv_heads, 2 * head_dim).transpose(0, 2, 1, 3)
    spread = spread.reshape(images * kv_heads, chunk, 2 * head_dim)
    held = lax.all_to_all(spread, DP + MP, split_axis=0, concat_axis=0, tiled=True)
    held = held.reshape(images, kv_heads * chunk, 2 * head_dim)
    target = jnp.arange(images, dtype=jnp.int32)
    wanted = jnp.stack([image_owner[jnp.maximum(target - 1, 0)], image_owner[target]], axis=1)
    selector = (wanted[:, :, None] == target[None, None, :]).astype(jnp.bfloat16)
    sent = jnp.einsum(
        "isn,ntd->istd", selector, held, preferred_element_type=jnp.float32
    ).astype(jnp.bfloat16)
    visual = lax.all_to_all(sent, DP, split_axis=0, concat_axis=0, tiled=True)
    which = jnp.clip(caption_image - here + 1, 0, 1).astype(jnp.int32)

    half = head_dim // 2
    length = rows // caption_image.shape[0]
    vis_tokens = tok_local * kv_heads
    freqs = ROPE_BASE ** (-jnp.arange(half, dtype=jnp.float32) / half)
    positions = (vis_tokens + jnp.arange(length, dtype=jnp.int32)).astype(jnp.float32)
    angles = positions[:, None] * freqs[None, :]
    cos = jnp.concatenate([jnp.cos(angles)] * 2, axis=1)
    sin = jnp.concatenate([-jnp.sin(angles), jnp.sin(angles)], axis=1)

    def tail(units):
        return pick(bias, units), cos, sin

    normed = norm_rows(tokens, norm_gain)
    turn = jnp.array([0, -1, 1, 2], jnp.int32)
    other = 1 - zl

    def line_of_b(plane, by):
        return plane * 16 + (x + by) % 4 * 4 + (y + turn) % 4

    def line_of_c(plane, by):
        return plane * 16 + (x + turn) % 4 * 4 + (y + by) % 4

    def ring_project(units, line_of, parts):
        early, later, final = parts
        acc = project(
            normed, jnp.concatenate([line_of(zl, 0), line_of(zl, -1), line_of(zl, 1)]), early
        )
        acc = project(
            normed,
            jnp.concatenate(
                [line_of(zl, 2), line_of(other, 0), line_of(other, -1), line_of(other, 1)]
            ),
            later,
            acc,
        )
        return project(normed, line_of(other, 2), [final], acc, units, tail(units))

    span = jnp.arange(16, dtype=jnp.int32)
    acc_d = project(normed, zl * 16 + span, [d_own])
    text = project(normed, other * 16 + span, [d_cross], acc_d, SET_D, tail(SET_D))
    q_b = ring_project(SET_B, line_of_b, parts_b)
    width = query_weight.shape[1]
    out = attend(which, caption_length, q_b, text, visual, 0, width)
    q_c = ring_project(SET_C, line_of_c, parts_c)
    return attend(which, caption_length, q_c, text, visual, 1, width, out)


def solution(mesh):
    grid = Mesh(mesh.devices.reshape(tuple(SIZES[a] for a in MESH_AXES)), MESH_AXES)
    placed = (
        P(DP, None),
        P(),
        P(DP, MP),
        P(MP),
        P(DP, MP, None),
        P(MP, None),
        P(DP, MP, None, None),
        P(DP),
        P(DP),
        P(),
    )
    return jax.shard_map(
        on_device, mesh=grid, in_specs=placed, out_specs=P(DP, MP), check_vma=False
    )
```

```python
import functools
import math

import jax
import jax.numpy as jnp
from jax import lax
from jax.experimental import pallas as pl
from jax.experimental.pallas import tpu as pltpu
from jax.sharding import Mesh
from jax.sharding import PartitionSpec as P

ROPE_BASE = 1000000.0
UNIT = 128
PIECE = 256
STEP = 1024
SET_D = (8, 9)
SET_B = (0, 1, 2, 3)
SET_C = (4, 5, 6, 7)
MESH_AXES = ("zl", "x", "y", "zh", "core")
SIZES = {"zl": 2, "x": 4, "y": 4, "zh": 2, "core": 2}
DP = ("zl", "x", "y")
MP = ("zh", "core")
PLANE = ("x", "y")
MIB = 2**20


def shift(value, axis, by):
    size = SIZES[axis]
    return lax.ppermute(value, axis, [(i, (i + by) % size) for i in range(size)])


def after(value, *others):
    return lax.optimization_barrier((value, others))[0]


def whole():
    return pl.BlockSpec(memory_space=pltpu.VMEM)


def norm_body(tokens_ref, gain_ref, out_ref):
    gain = gain_ref[...].astype(jnp.float32)
    for first in range(0, tokens_ref.shape[0], 16):
        rows = slice(first, first + 16)
        wide = tokens_ref[rows, :].astype(jnp.float32)
        mean_square = jnp.mean(wide * wide, -1, keepdims=True)
        normed = (wide * lax.rsqrt(mean_square + 1e-06) * gain).astype(jnp.bfloat16)
        for j in range(out_ref.shape[0]):
            out_ref[j, rows, :] = normed[:, j * PIECE : (j + 1) * PIECE]


def norm_rows(tokens, gain):
    rows, width = tokens.shape
    tile = 64
    return pl.pallas_call(
        norm_body,
        grid=(rows // tile,),
        in_specs=[
            pl.BlockSpec((tile, width), lambda i: (i, 0)),
            pl.BlockSpec((1, width), lambda i: (0, 0)),
        ],
        out_specs=pl.BlockSpec((width // PIECE, tile, PIECE), lambda i: (0, i, 0)),
        out_shape=jax.ShapeDtypeStruct((width // PIECE, rows, PIECE), jnp.bfloat16),
        compiler_params=pltpu.CompilerParams(vmem_limit_bytes=60 * MIB),
        cost_estimate=pl.CostEstimate(
            flops=4 * rows * width, bytes_accessed=4 * rows * width, transcendentals=rows
        ),
        name="norm_rows",
    )(tokens, gain.reshape(1, width))


def project_body(rows_of, has_acc, units, index_ref, x_ref, *refs):
    refs = list(refs)
    w_refs = [refs.pop(0) for _ in rows_of]
    acc_in = refs.pop(0) if has_acc else None
    if units:
        bias_ref, cos_ref, sin_ref = refs.pop(0), refs.pop(0), refs.pop(0)
    out_ref, w_buf, x_buf, acc, w_sems, x_sems, acc_sem = refs
    steps = sum(rows_of) // STEP
    each = STEP // PIECE
    slots = x_buf.shape[0]

    copies = [[] for _ in range(steps)]
    at = 0
    for ref, count in zip(w_refs, rows_of):
        done = 0
        while done < count:
            s, into = divmod(at, STEP)
            size = min(count - done, STEP - into)
            copies[s].append(
                pltpu.make_async_copy(
                    ref.at[pl.ds(done, size)],
                    w_buf.at[pl.ds(at, size)],
                    w_sems.at[s, len(copies[s])],
                )
            )
            done += size
            at += size

    def x_copies(s):
        return [
            pltpu.make_async_copy(
                x_ref.at[index_ref[each * s + j]], x_buf.at[s % slots, j], x_sems.at[s % slots, j]
            )
            for j in range(each)
        ]

    for s in range(steps):
        for copy in copies[s]:
            copy.start()
        if s < slots:
            for copy in x_copies(s):
                copy.start()
        if s == 0 and has_acc:
            load = pltpu.make_async_copy(acc_in, acc, acc_sem)
            load.start()

    tile = 256
    for s in range(steps):
        for copy in copies[s] + x_copies(s):
            copy.wait()
        if s == 0 and has_acc:
            load.wait()
        w = w_buf.at[pl.ds(s * STEP, STEP)]
        for m in range(0, acc.shape[0], tile):
            rows = slice(m, m + tile)
            x = jnp.concatenate([x_buf[s % slots, j, rows, :] for j in range(each)], axis=1)
            part = jnp.dot(x, w[...], preferred_element_type=jnp.float32)
            if s > 0 or has_acc:
                part += acc[rows, :]
            acc[rows, :] = part
        if s + slots < steps:
            for copy in x_copies(s + slots):
                copy.start()

    if units:

        def rope(i, carry):
            rows = pl.ds(pl.multiple_of(i * 64, 64), 64)
            for j, unit in enumerate(units):
                cols = slice(j * UNIT, (j + 1) * UNIT)
                value = acc[rows, cols] + bias_ref[:, cols]
                if unit != 9:
                    value = value * cos_ref[...] + pltpu.roll(value, 64, 1) * sin_ref[...]
                out_ref[rows, cols] = value.astype(jnp.bfloat16)
            return carry

        lax.fori_loop(0, out_ref.shape[0] // 64, rope, 0)
    else:
        store = pltpu.make_async_copy(acc, out_ref, acc_sem)
        store.start()
        store.wait()


def project(normed, index, weights, acc=None, units=None, tail=()):
    rows = normed.shape[1]
    width = weights[0].shape[1]
    rows_of = [w.shape[0] for w in weights]
    total = sum(rows_of)
    slots = min(3, total // STEP)
    accs = [] if acc is None else [acc]
    anywhere = pl.BlockSpec(memory_space=pl.ANY)
    return pl.pallas_call(
        functools.partial(project_body, rows_of, acc is not None, units),
        in_specs=[pl.BlockSpec(memory_space=pltpu.SMEM)]
        + [anywhere] * (1 + len(weights) + len(accs))
        + [whole()] * len(tail),
        out_specs=whole() if units else anywhere,
        out_shape=jax.ShapeDtypeStruct((rows, width), jnp.bfloat16 if units else jnp.float32),
        scratch_shapes=[
            pltpu.VMEM((total, width), jnp.bfloat16),
            pltpu.VMEM((slots, STEP // PIECE, rows, PIECE), jnp.bfloat16),
            pltpu.VMEM((rows, width), jnp.float32),
            pltpu.SemaphoreType.DMA((total // STEP, 4)),
            pltpu.SemaphoreType.DMA((slots, STEP // PIECE)),
            pltpu.SemaphoreType.DMA(()),
        ],
        compiler_params=pltpu.CompilerParams(vmem_limit_bytes=60 * MIB),
        cost_estimate=pl.CostEstimate(
            flops=2 * rows * total * width,
            bytes_accessed=2 * total * (width + rows) + 8 * rows * width,
            transcendentals=0,
        ),
        name="project",
    )(index, normed, *weights, *accs, *tail)


def attend_body(length, has_before, which_ref, len_ref, q_ref, text_ref, visual_ref, *refs):
    out_ref = refs[-1]
    now = pl.program_id(0)
    used = len_ref[now]
    heads = q_ref.shape[1] // UNIT
    factor = 1.0 / math.sqrt(UNIT) * math.log2(math.e)
    nt = (((1,), (1,)), ((), ()))

    def run(rows):
        query = jnp.concatenate(
            [q_ref[0:rows, j * UNIT : (j + 1) * UNIT] for j in range(heads)], axis=0
        )
        visual = visual_ref[...].reshape(-1, 2 * UNIT)
        text = text_ref[...]
        sv = lax.dot_general(query, visual[:, :UNIT], nt, preferred_element_type=jnp.float32)
        st = lax.dot_general(query, text[:, :UNIT], nt, preferred_element_type=jnp.float32)
        at = lax.broadcasted_iota(jnp.int32, st.shape, 0) % rows
        st = jnp.where(lax.broadcasted_iota(jnp.int32, st.shape, 1) <= at, st, -jnp.inf)
        top = jnp.maximum(jnp.max(sv, -1, keepdims=True), jnp.max(st, -1, keepdims=True))
        ev = jnp.exp2((sv - top) * factor)
        et = jnp.exp2((st - top) * factor)
        inverse = 1.0 / (jnp.sum(ev, -1, keepdims=True) + jnp.sum(et, -1, keepdims=True))
        pv = (ev * inverse).astype(jnp.bfloat16)
        pt = (et * inverse).astype(jnp.bfloat16)
        mixed = jnp.dot(pv, visual[:, UNIT:], preferred_element_type=jnp.float32)
        mixed += jnp.dot(pt, text[:, UNIT:], preferred_element_type=jnp.float32)
        keep = lax.broadcasted_iota(jnp.int32, (rows, UNIT), 0) < used
        for h in range(heads):
            out_ref[0:rows, h * UNIT : (h + 1) * UNIT] = jnp.where(
                keep, mixed[h * rows : (h + 1) * rows], 0.0
            ).astype(jnp.bfloat16)
        if rows < length:
            out_ref[rows:length, :] = jnp.zeros((length - rows, out_ref.shape[1]), jnp.bfloat16)

    for tile in range(1, length // 16 + 1):

        @pl.when((used > 16 * (tile - 1)) & (used <= 16 * tile))
        def _(tile=tile):
            run(16 * tile)


def attend(which, lengths, query, text, visual, place, out_width, before=None):
    captions = which.shape[0]
    rows, width = query.shape
    length = rows // captions
    relays, _, chunk, depth = visual.shape
    befores = [] if before is None else [before]
    return pl.pallas_call(
        functools.partial(attend_body, length, before is not None),
        grid_spec=pltpu.PrefetchScalarGridSpec(
            num_scalar_prefetch=2,
            grid=(captions,),
            in_specs=[
                pl.BlockSpec((length, width), lambda c, which, lens: (c, 0)),
                pl.BlockSpec((length, text.shape[1]), lambda c, which, lens: (c, 0)),
                pl.BlockSpec(
                    (relays, 1, chunk, depth), lambda c, which, lens: (0, which[c], 0, 0)
                ),
            ]
            + [pl.BlockSpec(memory_space=pl.ANY)] * len(befores),
            out_specs=pl.BlockSpec((length, width), lambda c, which, lens: (c, place)),
        ),
        out_shape=jax.ShapeDtypeStruct((rows, out_width), jnp.bfloat16),
        input_output_aliases={5: 0} if befores else {},
        compiler_params=pltpu.CompilerParams(vmem_limit_bytes=60 * MIB),
        cost_estimate=pl.CostEstimate(
            flops=4 * rows * width * relays * chunk,
            bytes_accessed=4 * rows * width,
            transcendentals=rows * (width // UNIT) * relays * chunk,
        ),
        name="attend",
    )(which, lengths, query, text, visual, *befores)


def line_gather(piece, axis):
    return jnp.concatenate(
        [piece, shift(piece, axis, 1), shift(piece, axis, -1), shift(piece, axis, 2)], axis=0
    )


def on_device(
    tokens,
    norm_gain,
    query_weight,
    query_bias,
    keyval_weight,
    keyval_bias,
    visual_keyval,
    caption_image,
    caption_length,
    image_owner,
):
    zl, x, y = (lax.axis_index(a) for a in DP)
    here = lax.axis_index(DP)
    rows = tokens.shape[0]
    depth = query_weight.shape[0]
    head_dim = keyval_weight.shape[2] // 2
    weight = jnp.concatenate([query_weight, keyval_weight.reshape(depth, -1)], axis=1)
    bias = jnp.concatenate([query_bias, keyval_bias.reshape(-1)]).astype(jnp.float32)[None]

    def pick(array, units):
        return array[:, units[0] * UNIT : (units[-1] + 1) * UNIT]

    w_d, w_b, w_c = (pick(weight, s) for s in (SET_D, SET_B, SET_C))

    d_own = lax.all_gather(w_d, PLANE, axis=0, tiled=True)
    cz = shift(w_c, "zl", 1)
    line_b = line_gather(w_b, "y")
    line_c = line_gather(w_c, "x")
    cross_c = line_gather(cz, "x")
    cross_b = shift(line_b, "zl", 1)

    tok_local = visual_keyval.shape[1]
    kv_heads = visual_keyval.shape[2]
    images = image_owner.shape[0]
    chunk = tok_local // images
    spread = visual_keyval.reshape(images, chunk, kv_heads, 2 * head_dim).transpose(0, 2, 1, 3)
    spread = spread.reshape(images * kv_heads, chunk, 2 * head_dim)
    held = lax.all_to_all(spread, DP + MP, split_axis=0, concat_axis=0, tiled=True)

    b_before, b_after = shift(line_b, "x", 1), shift(line_b, "x", -1)
    c_before, c_after = shift(line_c, "y", 1), shift(line_c, "y", -1)
    normed = norm_rows(tokens, after(norm_gain, line_b, line_c))

    cross_b, cross_c, b_before, b_after, c_before, c_after, held, d_own = (
        after(v, normed)
        for v in (cross_b, cross_c, b_before, b_after, c_before, c_after, held, d_own)
    )
    d_cross = shift(d_own, "zl", 1)
    cc_before, cc_after = shift(cross_c, "y", 1), shift(cross_c, "y", -1)
    cb_before, cb_after = shift(cross_b, "x", 1), shift(cross_b, "x", -1)
    b_far, c_far = shift(b_before, "x", 1), shift(c_before, "y", 1)

    held = held.reshape(images, kv_heads * chunk, 2 * head_dim)
    target = jnp.arange(images, dtype=jnp.int32)
    wanted = jnp.stack([image_owner[jnp.maximum(target - 1, 0)], image_owner[target]], axis=1)
    selector = (wanted[:, :, None] == target[None, None, :]).astype(jnp.bfloat16)
    sent = jnp.einsum(
        "isn,ntd->istd", selector, held, preferred_element_type=jnp.float32
    ).astype(jnp.bfloat16)
    visual = lax.all_to_all(sent, DP, split_axis=0, concat_axis=0, tiled=True)
    which = jnp.clip(caption_image - here + 1, 0, 1).astype(jnp.int32)

    half = head_dim // 2
    length = rows // caption_image.shape[0]
    vis_tokens = tok_local * kv_heads
    freqs = ROPE_BASE ** (-jnp.arange(half, dtype=jnp.float32) / half)
    positions = (vis_tokens + jnp.arange(length, dtype=jnp.int32)).astype(jnp.float32)
    angles = positions[:, None] * freqs[None, :]
    cos = jnp.concatenate([jnp.cos(angles)] * 2, axis=1)
    sin = jnp.concatenate([-jnp.sin(angles), jnp.sin(angles)], axis=1)

    def tail(units):
        return pick(bias, units), cos, sin

    turn = jnp.array([0, -1, 1, 2], jnp.int32)
    other = 1 - zl
    span = jnp.arange(16, dtype=jnp.int32)

    def lines_b(plane, *bys):
        return jnp.concatenate([plane * 16 + (x + by) % 4 * 4 + (y + turn) % 4 for by in bys])

    def lines_c(plane, *bys):
        return jnp.concatenate([plane * 16 + (x + turn) % 4 * 4 + (y + by) % 4 for by in bys])

    acc_b = project(normed, lines_b(zl, 0, -1, 1), [line_b, b_before, b_after])
    acc_c = project(normed, lines_c(zl, 0, -1, 1), [line_c, c_before, c_after])
    acc_d = project(normed, zl * 16 + span, [d_own])
    cb_before, cb_after, cc_before, cc_after, b_far, c_far = (
        after(v, acc_b, acc_c, acc_d)
        for v in (cb_before, cb_after, cc_before, cc_after, b_far, c_far)
    )
    cb_far, cc_far = shift(cb_after, "x", -1), shift(cc_after, "y", -1)
    acc_b = project(
        normed,
        jnp.concatenate([lines_b(zl, 2), lines_b(other, 0, -1, 1)]),
        [b_far, cross_b, cb_before, cb_after],
        acc_b,
    )
    acc_c = project(
        normed,
        jnp.concatenate([lines_c(zl, 2), lines_c(other, 0, -1, 1)]),
        [c_far, cross_c, cc_before, cc_after],
        acc_c,
    )
    cb_far, cc_far, d_cross, visual = (
        after(v, acc_b, acc_c) for v in (cb_far, cc_far, d_cross, visual)
    )
    text = project(normed, other * 16 + span, [d_cross], acc_d, SET_D, tail(SET_D))
    q_b = project(normed, lines_b(other, 2), [cb_far], acc_b, SET_B, tail(SET_B))
    width = query_weight.shape[1]
    out = attend(which, caption_length, q_b, text, visual, 0, width)
    q_c = project(normed, lines_c(other, 2), [cc_far], acc_c, SET_C, tail(SET_C))
    return attend(which, caption_length, q_c, text, visual, 1, width, out)


def solution(mesh):
    grid = Mesh(mesh.devices.reshape(tuple(SIZES[a] for a in MESH_AXES)), MESH_AXES)
    placed = (
        P(DP, None),
        P(),
        P(DP, MP),
        P(MP),
        P(DP, MP, None),
        P(MP, None),
        P(DP, MP, None, None),
        P(DP),
        P(DP),
        P(),
    )
    return jax.shard_map(
        on_device, mesh=grid, in_specs=placed, out_specs=P(DP, MP), check_vma=False
    )
```

```python
import functools
import math

import jax
import jax.numpy as jnp
import numpy as np
from jax import lax
from jax.experimental import pallas as pl
from jax.experimental.pallas import tpu as pltpu
from jax.sharding import Mesh
from jax.sharding import PartitionSpec as P

ROPE_BASE = 1000000.0
UNIT = 128
PIECE = 256
STEP = 1024
EACH = STEP // PIECE
KEYS, VALUES = 8, 9
SET_C = (8, 9, 0, 1, 2)
SET_B = (3, 4, 5, 6, 7)
MESH_AXES = ("zl", "x", "y", "zh", "core")
SIZES = {"zl": 2, "x": 4, "y": 4, "zh": 2, "core": 2}
DP = ("zl", "x", "y")
MP = ("zh", "core")
PLANE = ("x", "y")
MIB = 2**20


def shift(value, axis, by):
    size = SIZES[axis]
    return lax.ppermute(value, axis, [(i, (i + by) % size) for i in range(size)])


def after(value, *others):
    return lax.optimization_barrier((value, others))[0]


def whole():
    return pl.BlockSpec(memory_space=pltpu.VMEM)


def norm_body(late, tokens_ref, gain_ref, index_ref, out_ref, late_ref, buf, sems):
    rows = tokens_ref.shape[0]
    depth, tile = buf.shape[:2]
    count = rows // tile

    def copy(i, slot):
        at = pl.multiple_of(i * tile, tile)
        return pltpu.make_async_copy(tokens_ref.at[pl.ds(at, tile)], buf.at[slot], sems.at[slot])

    for i in range(depth - 1):
        copy(i, i).start()
    gain = gain_ref[...].astype(jnp.float32)

    def one(i, carry):
        slot = lax.rem(i, depth)

        @pl.when(i + depth - 1 < count)
        def _():
            copy(i + depth - 1, lax.rem(i + depth - 1, depth)).start()

        copy(i, slot).wait()
        for part in range(tile // 16):
            wide = buf[slot, part * 16 : (part + 1) * 16, :].astype(jnp.float32)
            mean_square = jnp.mean(wide * wide, -1, keepdims=True)
            out_ref[pl.ds(pl.multiple_of(i * tile + part * 16, 16), 16), :] = (
                wide * lax.rsqrt(mean_square + 1e-06) * gain
            ).astype(jnp.bfloat16)
        done = pl.ds(pl.multiple_of(i * tile, tile), tile)
        for j in range(EACH):
            piece = pl.ds(pl.multiple_of(index_ref[late + j] * PIECE, PIECE), PIECE)
            late_ref[done, j * PIECE : (j + 1) * PIECE] = out_ref[done, piece]
        return carry

    lax.fori_loop(0, count, one, 0)


def norm_rows(tokens, gain, index, late):
    rows, width = tokens.shape
    depth, tile = 4, 64
    return pl.pallas_call(
        functools.partial(norm_body, late),
        in_specs=[
            pl.BlockSpec(memory_space=pl.ANY),
            whole(),
            pl.BlockSpec(memory_space=pltpu.SMEM),
        ],
        out_specs=(whole(), whole()),
        out_shape=(
            jax.ShapeDtypeStruct((rows, width), jnp.bfloat16),
            jax.ShapeDtypeStruct((rows, STEP), jnp.bfloat16),
        ),
        scratch_shapes=[
            pltpu.VMEM((depth, tile, width), jnp.bfloat16),
            pltpu.SemaphoreType.DMA((depth,)),
        ],
        compiler_params=pltpu.CompilerParams(vmem_limit_bytes=24 * MIB),
        cost_estimate=pl.CostEstimate(
            flops=4 * rows * width, bytes_accessed=4 * rows * width, transcendentals=rows
        ),
        name="norm_rows",
    )(tokens, gain.reshape(1, width), index)


def project_body(rows_of, first, has_acc, units, index_ref, x_ref, *refs):
    refs = list(refs)
    w_refs = [refs.pop(0) for _ in rows_of]
    acc_in = refs.pop(0) if has_acc else None
    if units:
        bias_ref, cos_ref, sin_ref = refs.pop(0), refs.pop(0), refs.pop(0)
    out_ref, w_buf, sems = refs.pop(0), refs.pop(0), refs.pop(0)
    acc = refs.pop(0) if units else out_ref
    steps = sum(rows_of) // STEP

    copies = [[] for _ in range(steps)]
    at = 0
    for ref, count in zip(w_refs, rows_of):
        for done in range(0, count, STEP):
            s = at // STEP
            copies[s].append(
                pltpu.make_async_copy(
                    ref.at[pl.ds(done, STEP)], w_buf.at[pl.ds(at, STEP)], sems.at[s]
                )
            )
            at += STEP
    for group in copies:
        for copy in group:
            copy.start()

    tile = 256
    for s in range(steps):
        for copy in copies[s]:
            copy.wait()
        w = w_buf.at[pl.ds(s * STEP, STEP)]
        if first is None:
            cols = [slice((EACH * s + j) * PIECE, (EACH * s + j + 1) * PIECE) for j in range(EACH)]
        else:
            cols = [
                pl.ds(pl.multiple_of(index_ref[first + EACH * s + j] * PIECE, PIECE), PIECE)
                for j in range(EACH)
            ]
        for m in range(0, x_ref.shape[0], tile):
            x = jnp.concatenate([x_ref[m : m + tile, c] for c in cols], axis=1)
            part = jnp.dot(x, w[...], preferred_element_type=jnp.float32)
            if s > 0:
                part += acc[m : m + tile, :]
            elif has_acc:
                part += acc_in[m : m + tile, :]
            acc[m : m + tile, :] = part

    if units:

        def rope(i, carry):
            rows = pl.ds(pl.multiple_of(i * 64, 64), 64)
            for j, unit in enumerate(units):
                cols = slice(j * UNIT, (j + 1) * UNIT)
                value = acc[rows, cols] + bias_ref[:, unit * UNIT : (unit + 1) * UNIT]
                if unit != VALUES:
                    value = value * cos_ref[...] + pltpu.roll(value, 64, 1) * sin_ref[...]
                out_ref[rows, cols] = value.astype(jnp.bfloat16)
            return carry

        lax.fori_loop(0, out_ref.shape[0] // 64, rope, 0)


def project(normed, index, first, weights, acc=None, units=None, tail=()):
    rows = normed.shape[0]
    width = weights[0].shape[1]
    rows_of = [w.shape[0] for w in weights]
    total = sum(rows_of)
    scratch = [
        pltpu.VMEM((total, width), jnp.bfloat16),
        pltpu.SemaphoreType.DMA((total // STEP,)),
    ]
    if units:
        scratch.append(pltpu.VMEM((rows, width), jnp.float32))
    accs = [] if acc is None else [acc]
    return pl.pallas_call(
        functools.partial(project_body, rows_of, first, acc is not None, units),
        in_specs=[pl.BlockSpec(memory_space=pltpu.SMEM), whole()]
        + [pl.BlockSpec(memory_space=pl.ANY)] * len(weights)
        + [whole()] * (len(accs) + len(tail)),
        out_specs=whole(),
        out_shape=jax.ShapeDtypeStruct((rows, width), jnp.bfloat16 if units else jnp.float32),
        scratch_shapes=scratch,
        compiler_params=pltpu.CompilerParams(vmem_limit_bytes=20 * MIB),
        cost_estimate=pl.CostEstimate(
            flops=2 * rows * total * width, bytes_accessed=2 * total * width, transcendentals=0
        ),
        name="project",
    )(index, normed, *weights, *accs, *tail)


def attend_body(length, skip, which_ref, len_ref, q_ref, text_ref, visual_ref, *refs):
    out_ref = refs[-1]
    now = pl.program_id(0)
    used = len_ref[now]
    heads = q_ref.shape[1] // UNIT - skip
    factor = 1.0 / math.sqrt(UNIT) * math.log2(math.e)
    nt = (((1,), (1,)), ((), ()))
    before = 0
    if len(refs) > 1:
        before = refs[0].shape[1]
        out_ref[:, :before] = refs[0][...]

    def run(rows):
        query = jnp.concatenate(
            [q_ref[0:rows, j * UNIT : (j + 1) * UNIT] for j in range(skip, skip + heads)], axis=0
        )
        visual = visual_ref[...].reshape(-1, 2 * UNIT)
        text = text_ref[...]
        sv = lax.dot_general(query, visual[:, :UNIT], nt, preferred_element_type=jnp.float32)
        st = lax.dot_general(query, text[:, :UNIT], nt, preferred_element_type=jnp.float32)
        at = lax.broadcasted_iota(jnp.int32, st.shape, 0) % rows
        st = jnp.where(lax.broadcasted_iota(jnp.int32, st.shape, 1) <= at, st, -jnp.inf)
        top = jnp.maximum(jnp.max(sv, -1, keepdims=True), jnp.max(st, -1, keepdims=True))
        ev = jnp.exp2((sv - top) * factor)
        et = jnp.exp2((st - top) * factor)
        inverse = 1.0 / (jnp.sum(ev, -1, keepdims=True) + jnp.sum(et, -1, keepdims=True))
        pv = (ev * inverse).astype(jnp.bfloat16)
        pt = (et * inverse).astype(jnp.bfloat16)
        mixed = jnp.dot(pv, visual[:, UNIT:], preferred_element_type=jnp.float32)
        mixed += jnp.dot(pt, text[:, UNIT:], preferred_element_type=jnp.float32)
        keep = lax.broadcasted_iota(jnp.int32, (rows, UNIT), 0) < used
        for h in range(heads):
            out_ref[0:rows, before + h * UNIT : before + (h + 1) * UNIT] = jnp.where(
                keep, mixed[h * rows : (h + 1) * rows], 0.0
            ).astype(jnp.bfloat16)
        if rows < length:
            out_ref[rows:length, before:] = jnp.zeros((length - rows, heads * UNIT), jnp.bfloat16)

    for tile in range(1, length // 16 + 1):

        @pl.when((used > 16 * (tile - 1)) & (used <= 16 * tile))
        def _(tile=tile):
            run(16 * tile)


def attend(which, lengths, query, skip, text, visual, before=None):
    captions = which.shape[0]
    rows, width = query.shape
    length = rows // captions
    relays, _, chunk, depth = visual.shape
    befores = [] if before is None else [before]
    out_width = width - skip * UNIT + sum(b.shape[1] for b in befores)

    def by_caption(columns):
        return pl.BlockSpec((length, columns), lambda c, which, lens: (c, 0))

    return pl.pallas_call(
        functools.partial(attend_body, length, skip),
        grid_spec=pltpu.PrefetchScalarGridSpec(
            num_scalar_prefetch=2,
            grid=(captions,),
            in_specs=[
                by_caption(width),
                by_caption(2 * UNIT),
                pl.BlockSpec(
                    (relays, 1, chunk, depth), lambda c, which, lens: (0, which[c], 0, 0)
                ),
            ]
            + [by_caption(b.shape[1]) for b in befores],
            out_specs=by_caption(out_width),
        ),
        out_shape=jax.ShapeDtypeStruct((rows, out_width), jnp.bfloat16),
        compiler_params=pltpu.CompilerParams(vmem_limit_bytes=20 * MIB),
        cost_estimate=pl.CostEstimate(
            flops=4 * rows * width * relays * chunk,
            bytes_accessed=4 * rows * width,
            transcendentals=rows * (width // UNIT) * relays * chunk,
        ),
        name="attend",
    )(which, lengths, query, text, visual, *befores)


def line_gather(piece, axis):
    return jnp.concatenate(
        [piece, shift(piece, axis, 1), shift(piece, axis, -1), shift(piece, axis, 2)], axis=0
    )


def piece_table():
    turn = (0, -1, 1, 2)
    lines = [(0, 0), (0, -1), (0, 1), (1, 0), (0, 2), (1, -1), (1, 1), (1, 2)]
    ring_b = [(dz, by, t) for dz, by in lines for t in turn]
    ring_c = [(dz, t, by) for dz, by in lines for t in turn]
    return np.array(ring_b + ring_c, np.int32).T


def on_device(
    tokens,
    norm_gain,
    query_weight,
    query_bias,
    keyval_weight,
    keyval_bias,
    visual_keyval,
    caption_image,
    caption_length,
    image_owner,
):
    zl, x, y = (lax.axis_index(a) for a in DP)
    here = lax.axis_index(DP)
    rows = tokens.shape[0]
    depth = query_weight.shape[0]
    head_dim = keyval_weight.shape[2] // 2
    bias = jnp.concatenate([query_bias, keyval_bias.reshape(-1)]).astype(jnp.float32)[None]
    split = 3 * UNIT
    w_c = jnp.concatenate([keyval_weight.reshape(depth, -1), query_weight[:, :split]], axis=1)
    w_b = query_weight[:, split:]
    dz, dx, dy = piece_table()
    index = (zl + dz) % 2 * 16 + (x + dx) % 4 * 4 + (y + dy) % 4
    at_c = index.shape[0] // 2

    line_b = line_gather(w_b, "y")
    line_c = line_gather(w_c, "x")

    b_before, b_after = shift(line_b, "x", 1), shift(line_b, "x", -1)
    cross_b = shift(line_b, "zl", 1)
    c_before, c_after = shift(line_c, "y", 1), shift(line_c, "y", -1)

    tok_local = visual_keyval.shape[1]
    kv_heads = visual_keyval.shape[2]
    images = image_owner.shape[0]
    chunk = tok_local // images
    spread = visual_keyval.reshape(images, chunk, kv_heads, 2 * head_dim).transpose(0, 2, 1, 3)
    spread = spread.reshape(images * kv_heads, chunk, 2 * head_dim)
    held = lax.all_to_all(spread, DP + MP, split_axis=0, concat_axis=0, tiled=True)
    held = after(held, line_b, line_c)
    held = held.reshape(images, kv_heads * chunk, 2 * head_dim)
    wanted = jnp.stack([jnp.concatenate([image_owner[:1], image_owner[:-1]]), image_owner], axis=1)
    target = jnp.arange(images, dtype=jnp.int32)
    selector = (wanted[:, :, None] == target[None, None, :]).astype(jnp.bfloat16)
    sent = jnp.einsum(
        "isn,ntd->istd", selector, held, preferred_element_type=jnp.float32
    ).astype(jnp.bfloat16)
    visual = lax.all_to_all(sent, DP, split_axis=0, concat_axis=0, tiled=True)
    which = jnp.clip(caption_image - here + 1, 0, 1).astype(jnp.int32)

    half = head_dim // 2
    length = rows // caption_image.shape[0]
    freqs = ROPE_BASE ** (-np.arange(half, dtype=np.float64) / half)
    angles = (tok_local * kv_heads + np.arange(length))[:, None] * freqs[None, :]
    cos = np.concatenate([np.cos(angles)] * 2, axis=1).astype(np.float32)
    sin = np.concatenate([-np.sin(angles), np.sin(angles)], axis=1).astype(np.float32)
    tail = (bias, cos, sin)

    normed, normed_late = norm_rows(tokens, after(norm_gain, sent), index, 7 * EACH)
    b_before, b_after, cross_b, c_before, c_after, z_line_c = (
        after(v, normed) for v in (b_before, b_after, cross_b, c_before, c_after, line_c)
    )
    cross_c = shift(z_line_c, "zl", 1)
    b_far, c_far = shift(b_before, "x", 1), shift(c_before, "y", 1)
    cb_before, cb_after = shift(cross_b, "x", 1), shift(cross_b, "x", -1)
    acc_b = project(normed, index, 0, [line_b, b_before, b_after])
    acc_c = project(normed, index, at_c, [line_c, c_before, c_after])
    b_far, c_far, cross_c, cb_before, cb_after = (
        after(v, acc_b, acc_c) for v in (b_far, c_far, cross_c, cb_before, cb_after)
    )
    cc_before, cc_after = shift(cross_c, "y", 1), shift(cross_c, "y", -1)
    cc_far = shift(c_far, "zl", 1)
    cb_far = shift(cb_after, "x", -1)
    acc_b = project(normed, index, 3 * EACH, [cross_b, b_far], acc_b)
    acc_c = project(normed, index, at_c + 3 * EACH, [cross_c, c_far], acc_c)
    cb_before, cc_before, cc_after, cc_far = (
        after(v, acc_b, acc_c) for v in (cb_before, cc_before, cc_after, cc_far)
    )
    acc_b = project(normed, index, 5 * EACH, [cb_before, cb_after], acc_b)
    cc_before, cc_after, cc_far = (after(v, acc_b) for v in (cc_before, cc_after, cc_far))
    heads_c = project(
        normed, index, at_c + 5 * EACH, [cc_before, cc_after, cc_far], acc_c, SET_C, tail
    )
    visual, cb_far = (after(v, heads_c) for v in (visual, cb_far))
    out = attend(which, caption_length, heads_c, 2, heads_c, visual)
    cb_far = after(cb_far, out)
    heads_b = project(normed_late, index, None, [cb_far], acc_b, SET_B, tail)
    return attend(which, caption_length, heads_b, 0, heads_c, visual, out)


def solution(mesh):
    grid = Mesh(mesh.devices.reshape(tuple(SIZES[a] for a in MESH_AXES)), MESH_AXES)
    placed = (
        P(DP, None),
        P(),
        P(DP, MP),
        P(MP),
        P(DP, MP, None),
        P(MP, None),
        P(DP, MP, None, None),
        P(DP),
        P(DP),
        P(),
    )
    return jax.shard_map(
        on_device, mesh=grid, in_specs=placed, out_specs=P(DP, MP), check_vma=False
    )
```

```python
import functools
import math

import jax
import jax.numpy as jnp
import numpy as np
from jax import lax
from jax.experimental import pallas as pl
from jax.experimental.pallas import tpu as pltpu
from jax.sharding import Mesh
from jax.sharding import PartitionSpec as P

ROPE_BASE = 1000000.0
UNIT = 128
PIECE = 256
STEP = 1024
EACH = STEP // PIECE
TILE = 256
GROUP_ROWS = 256
KEYS, VALUES = 8, 9
SET_C = (8, 9, 0, 1, 2)
SET_B = (3, 4, 5, 6, 7)
MESH_AXES = ("zl", "x", "y", "zh", "core")
SIZES = {"zl": 2, "x": 4, "y": 4, "zh": 2, "core": 2}
DP = ("zl", "x", "y")
MP = ("zh", "core")
PLANE = ("x", "y")
MIB = 2**20


def shift(value, axis, by):
    size = SIZES[axis]
    return lax.ppermute(value, axis, [(i, (i + by) % size) for i in range(size)])


def after(value, *others):
    return lax.optimization_barrier((value, others))[0]


def whole():
    return pl.BlockSpec(memory_space=pltpu.VMEM)


def norm_body(late, tokens_ref, gain_ref, index_ref, out_ref, late_ref, buf, sems):
    rows = tokens_ref.shape[0]
    depth, tile = buf.shape[:2]
    count = rows // tile

    def copy(i, slot):
        at = pl.multiple_of(i * tile, tile)
        return pltpu.make_async_copy(tokens_ref.at[pl.ds(at, tile)], buf.at[slot], sems.at[slot])

    for i in range(depth - 1):
        copy(i, i).start()
    gain = gain_ref[...].astype(jnp.float32)

    def one(i, carry):
        slot = lax.rem(i, depth)

        @pl.when(i + depth - 1 < count)
        def _():
            copy(i + depth - 1, lax.rem(i + depth - 1, depth)).start()

        copy(i, slot).wait()
        for part in range(tile // 16):
            wide = buf[slot, part * 16 : (part + 1) * 16, :].astype(jnp.float32)
            mean_square = jnp.mean(wide * wide, -1, keepdims=True)
            out_ref[pl.ds(pl.multiple_of(i * tile + part * 16, 16), 16), :] = (
                wide * lax.rsqrt(mean_square + 1e-06) * gain
            ).astype(jnp.bfloat16)
        done = pl.ds(pl.multiple_of(i * tile, tile), tile)
        for j in range(EACH):
            piece = pl.ds(pl.multiple_of(index_ref[late + j] * PIECE, PIECE), PIECE)
            late_ref[done, j * PIECE : (j + 1) * PIECE] = out_ref[done, piece]
        return carry

    lax.fori_loop(0, count, one, 0)


def norm_rows(tokens, gain, index, late):
    rows, width = tokens.shape
    depth, tile = 4, 64
    return pl.pallas_call(
        functools.partial(norm_body, late),
        in_specs=[
            pl.BlockSpec(memory_space=pl.ANY),
            whole(),
            pl.BlockSpec(memory_space=pltpu.SMEM),
        ],
        out_specs=(whole(), whole()),
        out_shape=(
            jax.ShapeDtypeStruct((rows, width), jnp.bfloat16),
            jax.ShapeDtypeStruct((rows, STEP), jnp.bfloat16),
        ),
        scratch_shapes=[
            pltpu.VMEM((depth, tile, width), jnp.bfloat16),
            pltpu.SemaphoreType.DMA((depth,)),
        ],
        compiler_params=pltpu.CompilerParams(vmem_limit_bytes=24 * MIB),
        cost_estimate=pl.CostEstimate(flops=1, bytes_accessed=1, transcendentals=0),
        name="norm_rows",
    )(tokens, gain.reshape(1, width), index)


def project_body(rows_of, first, has_acc, units, index_ref, x_ref, *refs):
    refs = list(refs)
    w_refs = [refs.pop(0) for _ in rows_of]
    acc_in = refs.pop(0) if has_acc else None
    if units:
        bias_ref, cos_ref, sin_ref = refs.pop(0), refs.pop(0), refs.pop(0)
    out_ref, w_buf, sems = refs.pop(0), refs.pop(0), refs.pop(0)
    acc = refs.pop(0) if units else out_ref
    steps = sum(rows_of) // STEP

    copies = [[] for _ in range(steps)]
    at = 0
    for ref, count in zip(w_refs, rows_of):
        for done in range(0, count, STEP):
            s = at // STEP
            copies[s].append(
                pltpu.make_async_copy(
                    ref.at[pl.ds(done, STEP)], w_buf.at[pl.ds(at, STEP)], sems.at[s]
                )
            )
            at += STEP
    for group in copies:
        for copy in group:
            copy.start()

    tile = TILE
    for s in range(steps):
        for copy in copies[s]:
            copy.wait()
        w = w_buf.at[pl.ds(s * STEP, STEP)]
        if first is None:
            pieces = [
                slice((EACH * s + j) * PIECE, (EACH * s + j + 1) * PIECE) for j in range(EACH)
            ]
        else:
            pieces = [
                pl.ds(pl.multiple_of(index_ref[first + EACH * s + j] * PIECE, PIECE), PIECE)
                for j in range(EACH)
            ]
        for m in range(0, x_ref.shape[0], tile):
            x = jnp.concatenate([x_ref[m : m + tile, p] for p in pieces], axis=1)
            part = jnp.dot(x, w[...], preferred_element_type=jnp.float32)
            if s > 0:
                part += acc[m : m + tile, :]
            elif has_acc:
                part += acc_in[m : m + tile, :]
            if not units or s < steps - 1:
                acc[m : m + tile, :] = part
                continue
            for j, unit in enumerate(units):
                cols = slice(j * UNIT, (j + 1) * UNIT)
                value = part[:, cols] + bias_ref[:, unit * UNIT : (unit + 1) * UNIT]
                if unit != VALUES:
                    value = value * cos_ref[...] + pltpu.roll(value, UNIT // 2, 1) * sin_ref[...]
                out_ref[m : m + tile, cols] = value.astype(jnp.bfloat16)


def project(normed, index, first, weights, acc=None, units=None, tail=()):
    rows = normed.shape[0]
    width = weights[0].shape[1]
    rows_of = [w.shape[0] for w in weights]
    total = sum(rows_of)
    scratch = [
        pltpu.VMEM((total, width), jnp.bfloat16),
        pltpu.SemaphoreType.DMA((total // STEP,)),
    ]
    if units:
        scratch.append(pltpu.VMEM((rows, width), jnp.float32))
    accs = [] if acc is None else [acc]
    return pl.pallas_call(
        functools.partial(project_body, rows_of, first, acc is not None, units),
        in_specs=[pl.BlockSpec(memory_space=pltpu.SMEM), whole()]
        + [pl.BlockSpec(memory_space=pl.ANY)] * len(weights)
        + [whole()] * (len(accs) + len(tail)),
        out_specs=whole(),
        out_shape=jax.ShapeDtypeStruct((rows, width), jnp.bfloat16 if units else jnp.float32),
        scratch_shapes=scratch,
        compiler_params=pltpu.CompilerParams(vmem_limit_bytes=20 * MIB),
        cost_estimate=pl.CostEstimate(flops=1, bytes_accessed=1, transcendentals=0),
        name="project",
    )(index, normed, *weights, *accs, *tail)


def attend_body(length, skips, which_ref, len_ref, text_ref, visual_ref, *refs):
    out_ref = refs[-1]
    captions = which_ref.shape[0]
    units = [
        (ref, slice(j * UNIT, (j + 1) * UNIT))
        for ref, skip in zip(refs, skips)
        for j in range(skip, ref.shape[1] // UNIT)
    ]
    factor = 1.0 / math.sqrt(UNIT) * math.log2(math.e)
    nt = (((1,), (1,)), ((), ()))

    def run(now, used, rows):
        start = pl.multiple_of(now * length, length)
        here = pl.ds(start, rows)
        visual = visual_ref[:, which_ref[now]].reshape(-1, 2 * UNIT)
        text = text_ref[pl.ds(start, length), : 2 * UNIT]
        keep = lax.broadcasted_iota(jnp.int32, (rows, UNIT), 0) < used
        group = min(len(units), max(1, GROUP_ROWS // rows))
        for first in range(0, len(units), group):
            some = units[first : first + group]
            query = jnp.concatenate([ref[here, cols] for ref, cols in some], axis=0)
            sv = lax.dot_general(query, visual[:, :UNIT], nt, preferred_element_type=jnp.float32)
            st = lax.dot_general(query, text[:, :UNIT], nt, preferred_element_type=jnp.float32)
            at = lax.broadcasted_iota(jnp.int32, st.shape, 0) % rows
            st = jnp.where(lax.broadcasted_iota(jnp.int32, st.shape, 1) <= at, st, -jnp.inf)
            top = jnp.maximum(jnp.max(sv, -1, keepdims=True), jnp.max(st, -1, keepdims=True))
            ev = jnp.exp2((sv - top) * factor)
            et = jnp.exp2((st - top) * factor)
            inverse = 1.0 / (jnp.sum(ev, -1, keepdims=True) + jnp.sum(et, -1, keepdims=True))
            pv = (ev * inverse).astype(jnp.bfloat16)
            pt = (et * inverse).astype(jnp.bfloat16)
            mixed = jnp.dot(pv, visual[:, UNIT:], preferred_element_type=jnp.float32)
            mixed += jnp.dot(pt, text[:, UNIT:], preferred_element_type=jnp.float32)
            for h in range(len(some)):
                out_ref[here, (first + h) * UNIT : (first + h + 1) * UNIT] = jnp.where(
                    keep, mixed[h * rows : (h + 1) * rows], 0.0
                ).astype(jnp.bfloat16)
        if rows < length:
            out_ref[pl.ds(start + rows, length - rows), :] = jnp.zeros(
                (length - rows, out_ref.shape[1]), jnp.bfloat16
            )

    def caption(now, carry):
        used = len_ref[now]
        for tile in range(1, length // 16 + 1):

            @pl.when((used > 16 * (tile - 1)) & (used <= 16 * tile))
            def _(tile=tile):
                run(now, used, 16 * tile)

        return carry

    lax.fori_loop(0, captions, caption, 0)


def attend(which, lengths, text, visual, queries, skips):
    rows = text.shape[0]
    width = sum(q.shape[1] - s * UNIT for q, s in zip(queries, skips))
    return pl.pallas_call(
        functools.partial(attend_body, rows // which.shape[0], skips),
        in_specs=[pl.BlockSpec(memory_space=pltpu.SMEM)] * 2 + [whole()] * (2 + len(queries)),
        out_specs=whole(),
        out_shape=jax.ShapeDtypeStruct((rows, width), jnp.bfloat16),
        compiler_params=pltpu.CompilerParams(vmem_limit_bytes=24 * MIB),
        cost_estimate=pl.CostEstimate(flops=1, bytes_accessed=1, transcendentals=0),
        name="attend",
    )(which, lengths, text, visual, *queries)


def line_gather(piece, axis):
    return jnp.concatenate(
        [piece, shift(piece, axis, 1), shift(piece, axis, -1), shift(piece, axis, 2)], axis=0
    )


def piece_table():
    turn = (0, -1, 1, 2)
    lines = [(0, 0), (0, -1), (0, 1), (1, 0), (0, 2), (1, -1), (1, 1), (1, 2)]
    ring_b = [(dz, by, t) for dz, by in lines for t in turn]
    ring_c = [(dz, t, by) for dz, by in lines for t in turn]
    return np.array(ring_b + ring_c, np.int32).T


def on_device(
    tokens,
    norm_gain,
    query_weight,
    query_bias,
    keyval_weight,
    keyval_bias,
    visual_keyval,
    caption_image,
    caption_length,
    image_owner,
):
    zl, x, y = (lax.axis_index(a) for a in DP)
    here = lax.axis_index(DP)
    rows = tokens.shape[0]
    depth = query_weight.shape[0]
    head_dim = keyval_weight.shape[2] // 2
    bias = jnp.concatenate([query_bias, keyval_bias.reshape(-1)]).astype(jnp.float32)[None]
    split = 3 * UNIT
    w_c = jnp.concatenate([keyval_weight.reshape(depth, -1), query_weight[:, :split]], axis=1)
    w_b = query_weight[:, split:]
    dz, dx, dy = piece_table()
    index = (zl + dz) % 2 * 16 + (x + dx) % 4 * 4 + (y + dy) % 4
    at_c = index.shape[0] // 2

    line_b = line_gather(w_b, "y")
    line_c = line_gather(w_c, "x")

    b_before, b_after = shift(line_b, "x", 1), shift(line_b, "x", -1)
    cross_b = shift(line_b, "zl", 1)
    c_before, c_after = shift(line_c, "y", 1), shift(line_c, "y", -1)

    tok_local = visual_keyval.shape[1]
    kv_heads = visual_keyval.shape[2]
    half = head_dim // 2
    length = rows // caption_image.shape[0]
    freqs = ROPE_BASE ** (-np.arange(half, dtype=np.float64) / half)
    angles = (tok_local * kv_heads + np.arange(length))[:, None] * freqs[None, :]
    angles = np.tile(angles, (TILE // length, 1))
    cos = np.concatenate([np.cos(angles)] * 2, axis=1).astype(np.float32)
    sin = np.concatenate([-np.sin(angles), np.sin(angles)], axis=1).astype(np.float32)
    tail = (bias, cos, sin)

    normed, normed_late = norm_rows(tokens, after(norm_gain, line_b, line_c), index, 7 * EACH)
    b_before, b_after, cross_b, c_before, c_after, z_line_c = (
        after(v, normed) for v in (b_before, b_after, cross_b, c_before, c_after, line_c)
    )
    cross_c = shift(z_line_c, "zl", 1)
    b_far, c_far = shift(b_before, "x", 1), shift(c_before, "y", 1)
    cb_before, cb_after = shift(cross_b, "x", 1), shift(cross_b, "x", -1)
    acc_b = project(normed, index, 0, [line_b, b_before, b_after])
    acc_c = project(normed, index, at_c, [line_c, c_before, c_after])

    images = image_owner.shape[0]
    chunk = tok_local // images
    own_visual = after(visual_keyval, acc_b, acc_c)
    spread = own_visual.reshape(images, chunk, kv_heads, 2 * head_dim).transpose(0, 2, 1, 3)
    spread = spread.reshape(images * kv_heads, chunk, 2 * head_dim)
    held = lax.all_to_all(spread, DP + MP, split_axis=0, concat_axis=0, tiled=True)

    b_far, c_far, cross_c, cb_before, cb_after = (
        after(v, spread) for v in (b_far, c_far, cross_c, cb_before, cb_after)
    )
    cc_before, cc_after = shift(cross_c, "y", 1), shift(cross_c, "y", -1)
    cc_far = shift(c_far, "zl", 1)
    cb_far = shift(cb_after, "x", -1)

    held = after(held, cross_c, c_far, cb_after)
    held = held.reshape(images, kv_heads * chunk, 2 * head_dim)
    wanted = jnp.stack([jnp.concatenate([image_owner[:1], image_owner[:-1]]), image_owner], axis=1)
    target = jnp.arange(images, dtype=jnp.int32)
    selector = (wanted[:, :, None] == target[None, None, :]).astype(jnp.bfloat16)
    sent = jnp.einsum(
        "isn,ntd->istd", selector, held, preferred_element_type=jnp.float32
    ).astype(jnp.bfloat16)
    visual = lax.all_to_all(sent, DP, split_axis=0, concat_axis=0, tiled=True)
    which = jnp.clip(caption_image - here + 1, 0, 1).astype(jnp.int32)

    cross_b, cross_c = after(cross_b, sent), after(cross_c, sent)
    acc_b = project(normed, index, 3 * EACH, [cross_b, b_far, cb_before, cb_after], acc_b)
    acc_c = project(normed, index, at_c + 3 * EACH, [cross_c, c_far], acc_c)
    cc_before, cc_after, cc_far = (after(v, acc_b, acc_c) for v in (cc_before, cc_after, cc_far))
    heads_c = project(
        normed, index, at_c + 5 * EACH, [cc_before, cc_after, cc_far], acc_c, SET_C, tail
    )
    cb_far = after(cb_far, heads_c)
    heads_b = project(normed_late, index, None, [cb_far], acc_b, SET_B, tail)
    visual = after(visual, heads_b)
    return attend(which, caption_length, heads_c, visual, [heads_c, heads_b], (2, 0))


def solution(mesh):
    grid = Mesh(mesh.devices.reshape(tuple(SIZES[a] for a in MESH_AXES)), MESH_AXES)
    placed = (
        P(DP, None),
        P(),
        P(DP, MP),
        P(MP),
        P(DP, MP, None),
        P(MP, None),
        P(DP, MP, None, None),
        P(DP),
        P(DP),
        P(),
    )
    return jax.shard_map(
        on_device, mesh=grid, in_specs=placed, out_specs=P(DP, MP), check_vma=False
    )
```

```python
import functools
import math

import jax
import jax.numpy as jnp
import numpy as np
from jax import lax
from jax.experimental import pallas as pl
from jax.experimental.pallas import tpu as pltpu
from jax.sharding import Mesh
from jax.sharding import PartitionSpec as P

ROPE_BASE = 1000000.0
UNIT = 128
PIECE = 256
STEP = 1024
EACH = STEP // PIECE
TILE = 256
GROUP_ROWS = 256
KEYS, VALUES = 8, 9
SET_C = (8, 9, 0, 1, 2)
SET_B = (3, 4, 5, 6, 7)
MESH_AXES = ("zl", "x", "y", "zh", "core")
SIZES = {"zl": 2, "x": 4, "y": 4, "zh": 2, "core": 2}
DP = ("zl", "x", "y")
MP = ("zh", "core")
PLANE = ("x", "y")
MIB = 2**20


def shift(value, axis, by):
    size = SIZES[axis]
    return lax.ppermute(value, axis, [(i, (i + by) % size) for i in range(size)])


def after(value, *others):
    return lax.optimization_barrier((value, others))[0]


def whole():
    return pl.BlockSpec(memory_space=pltpu.VMEM)


def norm_body(late, tokens_ref, gain_ref, index_ref, out_ref, late_ref, buf, sems):
    rows = tokens_ref.shape[0]
    depth, tile = buf.shape[:2]
    count = rows // tile

    def copy(i, slot):
        at = pl.multiple_of(i * tile, tile)
        return pltpu.make_async_copy(tokens_ref.at[pl.ds(at, tile)], buf.at[slot], sems.at[slot])

    for i in range(depth - 1):
        copy(i, i).start()
    gain = gain_ref[...].astype(jnp.float32)

    def one(i, carry):
        slot = lax.rem(i, depth)

        @pl.when(i + depth - 1 < count)
        def _():
            copy(i + depth - 1, lax.rem(i + depth - 1, depth)).start()

        copy(i, slot).wait()
        for part in range(tile // 16):
            wide = buf[slot, part * 16 : (part + 1) * 16, :].astype(jnp.float32)
            mean_square = jnp.mean(wide * wide, -1, keepdims=True)
            out_ref[pl.ds(pl.multiple_of(i * tile + part * 16, 16), 16), :] = (
                wide * lax.rsqrt(mean_square + 1e-06) * gain
            ).astype(jnp.bfloat16)
        done = pl.ds(pl.multiple_of(i * tile, tile), tile)
        for j in range(late_ref.shape[1] // PIECE):
            piece = pl.ds(pl.multiple_of(index_ref[late + j] * PIECE, PIECE), PIECE)
            late_ref[done, j * PIECE : (j + 1) * PIECE] = out_ref[done, piece]
        return carry

    lax.fori_loop(0, count, one, 0)


def norm_rows(tokens, gain, index, late):
    rows, width = tokens.shape
    depth, tile = 4, 64
    return pl.pallas_call(
        functools.partial(norm_body, late),
        in_specs=[
            pl.BlockSpec(memory_space=pl.ANY),
            whole(),
            pl.BlockSpec(memory_space=pltpu.SMEM),
        ],
        out_specs=(whole(), whole()),
        out_shape=(
            jax.ShapeDtypeStruct((rows, width), jnp.bfloat16),
            jax.ShapeDtypeStruct((rows, 2 * STEP), jnp.bfloat16),
        ),
        scratch_shapes=[
            pltpu.VMEM((depth, tile, width), jnp.bfloat16),
            pltpu.SemaphoreType.DMA((depth,)),
        ],
        compiler_params=pltpu.CompilerParams(vmem_limit_bytes=24 * MIB),
        cost_estimate=pl.CostEstimate(flops=1, bytes_accessed=1, transcendentals=0),
        name="norm_rows",
    )(tokens, gain.reshape(1, width), index)


def project_body(rows_of, first, has_acc, units, index_ref, x_ref, *refs):
    refs = list(refs)
    w_refs = [refs.pop(0) for _ in rows_of]
    acc_in = refs.pop(0) if has_acc else None
    if units:
        bias_ref, cos_ref, sin_ref = refs.pop(0), refs.pop(0), refs.pop(0)
    out_ref, w_buf, sems = refs.pop(0), refs.pop(0), refs.pop(0)
    acc = refs.pop(0) if units else out_ref
    steps = sum(rows_of) // STEP

    copies = [[] for _ in range(steps)]
    at = 0
    for ref, count in zip(w_refs, rows_of):
        for done in range(0, count, STEP):
            s = at // STEP
            copies[s].append(
                pltpu.make_async_copy(
                    ref.at[pl.ds(done, STEP)], w_buf.at[pl.ds(at, STEP)], sems.at[s]
                )
            )
            at += STEP
    for group in copies:
        for copy in group:
            copy.start()

    tile = TILE
    for s in range(steps):
        for copy in copies[s]:
            copy.wait()
        w = w_buf.at[pl.ds(s * STEP, STEP)]
        if first is None:
            pieces = [
                slice((EACH * s + j) * PIECE, (EACH * s + j + 1) * PIECE) for j in range(EACH)
            ]
        else:
            pieces = [
                pl.ds(pl.multiple_of(index_ref[first + EACH * s + j] * PIECE, PIECE), PIECE)
                for j in range(EACH)
            ]
        for m in range(0, x_ref.shape[0], tile):
            x = jnp.concatenate([x_ref[m : m + tile, p] for p in pieces], axis=1)
            part = jnp.dot(x, w[...], preferred_element_type=jnp.float32)
            if s > 0:
                part += acc[m : m + tile, :]
            elif has_acc:
                part += acc_in[m : m + tile, :]
            if not units or s < steps - 1:
                acc[m : m + tile, :] = part
                continue
            for j, unit in enumerate(units):
                cols = slice(j * UNIT, (j + 1) * UNIT)
                value = part[:, cols] + bias_ref[:, unit * UNIT : (unit + 1) * UNIT]
                if unit != VALUES:
                    value = value * cos_ref[...] + pltpu.roll(value, UNIT // 2, 1) * sin_ref[...]
                out_ref[m : m + tile, cols] = value.astype(jnp.bfloat16)


def project(normed, index, first, weights, acc=None, units=None, tail=()):
    rows = normed.shape[0]
    width = weights[0].shape[1]
    rows_of = [w.shape[0] for w in weights]
    total = sum(rows_of)
    scratch = [
        pltpu.VMEM((total, width), jnp.bfloat16),
        pltpu.SemaphoreType.DMA((total // STEP,)),
    ]
    if units:
        scratch.append(pltpu.VMEM((rows, width), jnp.float32))
    accs = [] if acc is None else [acc]
    return pl.pallas_call(
        functools.partial(project_body, rows_of, first, acc is not None, units),
        in_specs=[pl.BlockSpec(memory_space=pltpu.SMEM), whole()]
        + [pl.BlockSpec(memory_space=pl.ANY)] * len(weights)
        + [whole()] * (len(accs) + len(tail)),
        out_specs=whole(),
        out_shape=jax.ShapeDtypeStruct((rows, width), jnp.bfloat16 if units else jnp.float32),
        scratch_shapes=scratch,
        compiler_params=pltpu.CompilerParams(vmem_limit_bytes=20 * MIB),
        cost_estimate=pl.CostEstimate(flops=1, bytes_accessed=1, transcendentals=0),
        name="project",
    )(index, normed, *weights, *accs, *tail)


def attend_body(length, skips, which_ref, len_ref, text_ref, visual_ref, *refs):
    out_ref = refs[-1]
    captions = which_ref.shape[0]
    units = [
        (ref, slice(j * UNIT, (j + 1) * UNIT))
        for ref, skip in zip(refs, skips)
        for j in range(skip, ref.shape[1] // UNIT)
    ]
    factor = 1.0 / math.sqrt(UNIT) * math.log2(math.e)
    nt = (((1,), (1,)), ((), ()))

    def run(now, used, rows):
        start = pl.multiple_of(now * length, length)
        here = pl.ds(start, rows)
        visual = visual_ref[:, which_ref[now]].reshape(-1, 2 * UNIT)
        text = text_ref[pl.ds(start, length), : 2 * UNIT]
        keep = lax.broadcasted_iota(jnp.int32, (rows, UNIT), 0) < used
        group = min(len(units), max(1, GROUP_ROWS // rows))
        groups = [units[first : first + group] for first in range(0, len(units), group)]

        def scores(some):
            query = jnp.concatenate([ref[here, cols] for ref, cols in some], axis=0)
            return (
                lax.dot_general(query, visual[:, :UNIT], nt, preferred_element_type=jnp.float32),
                lax.dot_general(query, text[:, :UNIT], nt, preferred_element_type=jnp.float32),
            )

        coming = scores(groups[0])
        for i, some in enumerate(groups):
            first = i * group
            sv, st = coming
            if i + 1 < len(groups):
                coming = scores(groups[i + 1])
            at = lax.broadcasted_iota(jnp.int32, st.shape, 0) % rows
            st = jnp.where(lax.broadcasted_iota(jnp.int32, st.shape, 1) <= at, st, -jnp.inf)
            top = jnp.maximum(jnp.max(sv, -1, keepdims=True), jnp.max(st, -1, keepdims=True))
            ev = jnp.exp2((sv - top) * factor)
            et = jnp.exp2((st - top) * factor)
            inverse = 1.0 / (jnp.sum(ev, -1, keepdims=True) + jnp.sum(et, -1, keepdims=True))
            pv = (ev * inverse).astype(jnp.bfloat16)
            pt = (et * inverse).astype(jnp.bfloat16)
            mixed = jnp.dot(pv, visual[:, UNIT:], preferred_element_type=jnp.float32)
            mixed += jnp.dot(pt, text[:, UNIT:], preferred_element_type=jnp.float32)
            for h in range(len(some)):
                out_ref[here, (first + h) * UNIT : (first + h + 1) * UNIT] = jnp.where(
                    keep, mixed[h * rows : (h + 1) * rows], 0.0
                ).astype(jnp.bfloat16)
        if rows < length:
            out_ref[pl.ds(start + rows, length - rows), :] = jnp.zeros(
                (length - rows, out_ref.shape[1]), jnp.bfloat16
            )

    def caption(now, carry):
        used = len_ref[now]
        for tile in range(1, length // 16 + 1):

            @pl.when((used > 16 * (tile - 1)) & (used <= 16 * tile))
            def _(tile=tile):
                run(now, used, 16 * tile)

        return carry

    lax.fori_loop(0, captions, caption, 0)


def attend(which, lengths, text, visual, queries, skips):
    rows = text.shape[0]
    width = sum(q.shape[1] - s * UNIT for q, s in zip(queries, skips))
    return pl.pallas_call(
        functools.partial(attend_body, rows // which.shape[0], skips),
        in_specs=[pl.BlockSpec(memory_space=pltpu.SMEM)] * 2 + [whole()] * (2 + len(queries)),
        out_specs=whole(),
        out_shape=jax.ShapeDtypeStruct((rows, width), jnp.bfloat16),
        compiler_params=pltpu.CompilerParams(vmem_limit_bytes=24 * MIB),
        cost_estimate=pl.CostEstimate(flops=1, bytes_accessed=1, transcendentals=0),
        name="attend",
    )(which, lengths, text, visual, *queries)


def line_gather(piece, axis):
    return jnp.concatenate(
        [piece, shift(piece, axis, 1), shift(piece, axis, -1), shift(piece, axis, 2)], axis=0
    )


def piece_table():
    turn = (0, -1, 1, 2)
    lines_b = [(0, 0), (0, -1), (0, 1), (1, 0), (1, -1), (1, 1), (0, 2), (1, 2)]
    lines_c = [(0, 0), (0, -1), (0, 1), (1, 0), (0, 2), (1, -1), (1, 1), (1, 2)]
    ring_b = [(dz, by, t) for dz, by in lines_b for t in turn]
    ring_c = [(dz, t, by) for dz, by in lines_c for t in turn]
    return np.array(ring_b + ring_c, np.int32).T


def on_device(
    tokens,
    norm_gain,
    query_weight,
    query_bias,
    keyval_weight,
    keyval_bias,
    visual_keyval,
    caption_image,
    caption_length,
    image_owner,
):
    zl, x, y = (lax.axis_index(a) for a in DP)
    here = lax.axis_index(DP)
    rows = tokens.shape[0]
    depth = query_weight.shape[0]
    head_dim = keyval_weight.shape[2] // 2
    bias = jnp.concatenate([query_bias, keyval_bias.reshape(-1)]).astype(jnp.float32)[None]
    split = 3 * UNIT
    w_c = jnp.concatenate([keyval_weight.reshape(depth, -1), query_weight[:, :split]], axis=1)
    w_b = query_weight[:, split:]
    dz, dx, dy = piece_table()
    index = (zl + dz) % 2 * 16 + (x + dx) % 4 * 4 + (y + dy) % 4
    at_c = index.shape[0] // 2

    line_b = line_gather(w_b, "y")
    line_c = line_gather(w_c, "x")

    b_before, b_after = shift(line_b, "x", 1), shift(line_b, "x", -1)
    cross_b = shift(line_b, "zl", 1)
    c_before, c_after = shift(line_c, "y", 1), shift(line_c, "y", -1)

    tok_local = visual_keyval.shape[1]
    kv_heads = visual_keyval.shape[2]
    half = head_dim // 2
    length = rows // caption_image.shape[0]
    freqs = ROPE_BASE ** (-np.arange(half, dtype=np.float64) / half)
    angles = (tok_local * kv_heads + np.arange(length))[:, None] * freqs[None, :]
    angles = np.tile(angles, (TILE // length, 1))
    cos = np.concatenate([np.cos(angles)] * 2, axis=1).astype(np.float32)
    sin = np.concatenate([-np.sin(angles), np.sin(angles)], axis=1).astype(np.float32)
    tail = (bias, cos, sin)

    normed, normed_late = norm_rows(tokens, after(norm_gain, line_b, line_c), index, 6 * EACH)
    b_before, b_after, cross_b, c_before, c_after, z_line_c = (
        after(v, normed) for v in (b_before, b_after, cross_b, c_before, c_after, line_c)
    )
    cross_c = shift(z_line_c, "zl", 1)
    b_far, c_far = shift(b_before, "x", 1), shift(c_before, "y", 1)
    cb_before, cb_after = shift(cross_b, "x", 1), shift(cross_b, "x", -1)
    acc_b = project(normed, index, 0, [line_b, b_before, b_after])
    acc_c = project(normed, index, at_c, [line_c, c_before, c_after])

    images = image_owner.shape[0]
    chunk = tok_local // images
    own_visual = after(visual_keyval, acc_b, acc_c)
    spread = own_visual.reshape(images, chunk, kv_heads, 2 * head_dim).transpose(0, 2, 1, 3)
    spread = spread.reshape(images * kv_heads, chunk, 2 * head_dim)
    held = lax.all_to_all(spread, DP + MP, split_axis=0, concat_axis=0, tiled=True)

    b_far, c_far, cross_c, cb_before, cb_after = (
        after(v, spread) for v in (b_far, c_far, cross_c, cb_before, cb_after)
    )
    cc_before, cc_after = shift(cross_c, "y", 1), shift(cross_c, "y", -1)
    cc_far = shift(c_far, "zl", 1)
    cb_far = shift(cb_after, "x", -1)

    held = after(held, cross_c, c_far, cb_after)
    held = held.reshape(images, kv_heads * chunk, 2 * head_dim)
    wanted = jnp.stack([jnp.concatenate([image_owner[:1], image_owner[:-1]]), image_owner], axis=1)
    target = jnp.arange(images, dtype=jnp.int32)
    selector = (wanted[:, :, None] == target[None, None, :]).astype(jnp.bfloat16)
    sent = jnp.einsum(
        "isn,ntd->istd", selector, held, preferred_element_type=jnp.float32
    ).astype(jnp.bfloat16)
    visual = lax.all_to_all(sent, DP, split_axis=0, concat_axis=0, tiled=True)
    which = jnp.clip(caption_image - here + 1, 0, 1).astype(jnp.int32)

    cross_c = after(cross_c, sent)
    acc_c = project(normed, index, at_c + 3 * EACH, [cross_c, c_far], acc_c)
    cross_b = after(cross_b, acc_c)
    acc_b = project(normed, index, 3 * EACH, [cross_b, cb_before, cb_after], acc_b)
    cc_before, cc_after, cc_far = (after(v, acc_b, acc_c) for v in (cc_before, cc_after, cc_far))
    heads_c = project(
        normed, index, at_c + 5 * EACH, [cc_before, cc_after, cc_far], acc_c, SET_C, tail
    )
    b_far, cb_far = after(b_far, heads_c), after(cb_far, heads_c)
    heads_b = project(normed_late, index, None, [b_far, cb_far], acc_b, SET_B, tail)
    visual = after(visual, heads_b)
    return attend(which, caption_length, heads_c, visual, [heads_c, heads_b], (2, 0))


def solution(mesh):
    grid = Mesh(mesh.devices.reshape(tuple(SIZES[a] for a in MESH_AXES)), MESH_AXES)
    placed = (
        P(DP, None),
        P(),
        P(DP, MP),
        P(MP),
        P(DP, MP, None),
        P(MP, None),
        P(DP, MP, None, None),
        P(DP),
        P(DP),
        P(),
    )
    return jax.shard_map(
        on_device, mesh=grid, in_specs=placed, out_specs=P(DP, MP), check_vma=False
    )
```

```python
import functools
import math

import jax
import jax.numpy as jnp
import numpy as np
from jax import lax
from jax.experimental import pallas as pl
from jax.experimental.pallas import tpu as pltpu
from jax.sharding import Mesh
from jax.sharding import PartitionSpec as P

ROPE_BASE = 1000000.0
UNIT = 128
PIECE = 256
STEP = 1024
EACH = STEP // PIECE
TILE = 256
GROUP_ROWS = 256
KEYS, VALUES = 8, 9
SET_C = (8, 9, 0, 1, 2)
SET_B = (3, 4, 5, 6, 7)
MESH_AXES = ("zl", "x", "y", "zh", "core")
SIZES = {"zl": 2, "x": 4, "y": 4, "zh": 2, "core": 2}
DP = ("zl", "x", "y")
MP = ("zh", "core")
PLANE = ("x", "y")
MIB = 2**20


def shift(value, axis, by):
    size = SIZES[axis]
    return lax.ppermute(value, axis, [(i, (i + by) % size) for i in range(size)])


def after(value, *others):
    return lax.optimization_barrier((value, others))[0]


def whole():
    return pl.BlockSpec(memory_space=pltpu.VMEM)


def norm_body(late, tokens_ref, gain_ref, index_ref, out_ref, late_ref, buf, sems):
    rows = tokens_ref.shape[0]
    depth, tile = buf.shape[:2]
    count = rows // tile

    def copy(i, slot):
        at = pl.multiple_of(i * tile, tile)
        return pltpu.make_async_copy(tokens_ref.at[pl.ds(at, tile)], buf.at[slot], sems.at[slot])

    for i in range(depth - 1):
        copy(i, i).start()
    gain = gain_ref[...].astype(jnp.float32)

    def one(i, carry):
        slot = lax.rem(i, depth)

        @pl.when(i + depth - 1 < count)
        def _():
            copy(i + depth - 1, lax.rem(i + depth - 1, depth)).start()

        copy(i, slot).wait()
        for part in range(tile // 16):
            wide = buf[slot, part * 16 : (part + 1) * 16, :].astype(jnp.float32)
            mean_square = jnp.mean(wide * wide, -1, keepdims=True)
            out_ref[pl.ds(pl.multiple_of(i * tile + part * 16, 16), 16), :] = (
                wide * lax.rsqrt(mean_square + 1e-06) * gain
            ).astype(jnp.bfloat16)
        done = pl.ds(pl.multiple_of(i * tile, tile), tile)
        for j in range(EACH):
            piece = pl.ds(pl.multiple_of(index_ref[late + j] * PIECE, PIECE), PIECE)
            late_ref[done, j * PIECE : (j + 1) * PIECE] = out_ref[done, piece]
        return carry

    lax.fori_loop(0, count, one, 0)


def norm_rows(tokens, gain, index, late):
    rows, width = tokens.shape
    depth, tile = 4, 64
    return pl.pallas_call(
        functools.partial(norm_body, late),
        in_specs=[
            pl.BlockSpec(memory_space=pl.ANY),
            whole(),
            pl.BlockSpec(memory_space=pltpu.SMEM),
        ],
        out_specs=(whole(), whole()),
        out_shape=(
            jax.ShapeDtypeStruct((rows, width), jnp.bfloat16),
            jax.ShapeDtypeStruct((rows, STEP), jnp.bfloat16),
        ),
        scratch_shapes=[
            pltpu.VMEM((depth, tile, width), jnp.bfloat16),
            pltpu.SemaphoreType.DMA((depth,)),
        ],
        compiler_params=pltpu.CompilerParams(vmem_limit_bytes=24 * MIB),
        cost_estimate=pl.CostEstimate(flops=1, bytes_accessed=1, transcendentals=0),
        name="norm_rows",
    )(tokens, gain.reshape(1, width), index)


def project_body(rows_of, first, has_acc, units, index_ref, x_ref, *refs):
    refs = list(refs)
    w_refs = [refs.pop(0) for _ in rows_of]
    acc_in = refs.pop(0) if has_acc else None
    if units:
        bias_ref, cos_ref, sin_ref = refs.pop(0), refs.pop(0), refs.pop(0)
    out_ref, w_buf, sems = refs.pop(0), refs.pop(0), refs.pop(0)
    acc = refs.pop(0) if units else out_ref
    steps = sum(rows_of) // STEP

    copies = [[] for _ in range(steps)]
    at = 0
    for ref, count in zip(w_refs, rows_of):
        for done in range(0, count, STEP):
            s = at // STEP
            copies[s].append(
                pltpu.make_async_copy(
                    ref.at[pl.ds(done, STEP)], w_buf.at[pl.ds(at, STEP)], sems.at[s]
                )
            )
            at += STEP
    for group in copies:
        for copy in group:
            copy.start()

    tile = TILE
    for s in range(steps):
        for copy in copies[s]:
            copy.wait()
        w = w_buf.at[pl.ds(s * STEP, STEP)]
        if first is None:
            pieces = [
                slice((EACH * s + j) * PIECE, (EACH * s + j + 1) * PIECE) for j in range(EACH)
            ]
        else:
            pieces = [
                pl.ds(pl.multiple_of(index_ref[first + EACH * s + j] * PIECE, PIECE), PIECE)
                for j in range(EACH)
            ]
        for m in range(0, x_ref.shape[0], tile):
            x = jnp.concatenate([x_ref[m : m + tile, p] for p in pieces], axis=1)
            part = jnp.dot(x, w[...], preferred_element_type=jnp.float32)
            if s > 0:
                part += acc[m : m + tile, :]
            elif has_acc:
                part += acc_in[m : m + tile, :]
            if not units or s < steps - 1:
                acc[m : m + tile, :] = part
                continue
            for j, unit in enumerate(units):
                cols = slice(j * UNIT, (j + 1) * UNIT)
                value = part[:, cols] + bias_ref[:, unit * UNIT : (unit + 1) * UNIT]
                if unit != VALUES:
                    value = value * cos_ref[...] + pltpu.roll(value, UNIT // 2, 1) * sin_ref[...]
                out_ref[m : m + tile, cols] = value.astype(jnp.bfloat16)


def project(normed, index, first, weights, acc=None, units=None, tail=()):
    rows = normed.shape[0]
    width = weights[0].shape[1]
    rows_of = [w.shape[0] for w in weights]
    total = sum(rows_of)
    scratch = [
        pltpu.VMEM((total, width), jnp.bfloat16),
        pltpu.SemaphoreType.DMA((total // STEP,)),
    ]
    if units:
        scratch.append(pltpu.VMEM((rows, width), jnp.float32))
    accs = [] if acc is None else [acc]
    return pl.pallas_call(
        functools.partial(project_body, rows_of, first, acc is not None, units),
        in_specs=[pl.BlockSpec(memory_space=pltpu.SMEM), whole()]
        + [pl.BlockSpec(memory_space=pl.ANY)] * len(weights)
        + [whole()] * (len(accs) + len(tail)),
        out_specs=whole(),
        out_shape=jax.ShapeDtypeStruct((rows, width), jnp.bfloat16 if units else jnp.float32),
        scratch_shapes=scratch,
        compiler_params=pltpu.CompilerParams(vmem_limit_bytes=20 * MIB),
        cost_estimate=pl.CostEstimate(flops=1, bytes_accessed=1, transcendentals=0),
        name="project",
    )(index, normed, *weights, *accs, *tail)


def attend_body(length, skips, which_ref, len_ref, text_ref, visual_ref, *refs):
    out_ref = refs[-1]
    captions = which_ref.shape[0]
    units = [
        (ref, slice(j * UNIT, (j + 1) * UNIT))
        for ref, skip in zip(refs, skips)
        for j in range(skip, ref.shape[1] // UNIT)
    ]
    factor = 1.0 / math.sqrt(UNIT) * math.log2(math.e)
    nt = (((1,), (1,)), ((), ()))

    def run(now, used, rows):
        start = pl.multiple_of(now * length, length)
        here = pl.ds(start, rows)
        visual = visual_ref[:, which_ref[now]].reshape(-1, 2 * UNIT)
        text = text_ref[pl.ds(start, length), : 2 * UNIT]
        keep = lax.broadcasted_iota(jnp.int32, (rows, UNIT), 0) < used
        group = min(len(units), max(1, GROUP_ROWS // rows))
        groups = [units[first : first + group] for first in range(0, len(units), group)]

        def scores(some):
            query = jnp.concatenate([ref[here, cols] for ref, cols in some], axis=0)
            return (
                lax.dot_general(query, visual[:, :UNIT], nt, preferred_element_type=jnp.float32),
                lax.dot_general(query, text[:, :UNIT], nt, preferred_element_type=jnp.float32),
            )

        coming = scores(groups[0])
        for i, some in enumerate(groups):
            first = i * group
            sv, st = coming
            if i + 1 < len(groups):
                coming = scores(groups[i + 1])
            at = lax.broadcasted_iota(jnp.int32, st.shape, 0) % rows
            st = jnp.where(lax.broadcasted_iota(jnp.int32, st.shape, 1) <= at, st, -jnp.inf)
            top = jnp.maximum(jnp.max(sv, -1, keepdims=True), jnp.max(st, -1, keepdims=True))
            ev = jnp.exp2((sv - top) * factor)
            et = jnp.exp2((st - top) * factor)
            inverse = 1.0 / (jnp.sum(ev, -1, keepdims=True) + jnp.sum(et, -1, keepdims=True))
            pv = (ev * inverse).astype(jnp.bfloat16)
            pt = (et * inverse).astype(jnp.bfloat16)
            mixed = jnp.dot(pv, visual[:, UNIT:], preferred_element_type=jnp.float32)
            mixed += jnp.dot(pt, text[:, UNIT:], preferred_element_type=jnp.float32)
            for h in range(len(some)):
                out_ref[here, (first + h) * UNIT : (first + h + 1) * UNIT] = jnp.where(
                    keep, mixed[h * rows : (h + 1) * rows], 0.0
                ).astype(jnp.bfloat16)
        if rows < length:
            out_ref[pl.ds(start + rows, length - rows), :] = jnp.zeros(
                (length - rows, out_ref.shape[1]), jnp.bfloat16
            )

    def caption(now, carry):
        used = len_ref[now]
        for tile in range(1, length // 16 + 1):

            @pl.when((used > 16 * (tile - 1)) & (used <= 16 * tile))
            def _(tile=tile):
                run(now, used, 16 * tile)

        return carry

    lax.fori_loop(0, captions, caption, 0)


def attend(which, lengths, text, visual, queries, skips):
    rows = text.shape[0]
    width = sum(q.shape[1] - s * UNIT for q, s in zip(queries, skips))
    return pl.pallas_call(
        functools.partial(attend_body, rows // which.shape[0], skips),
        in_specs=[pl.BlockSpec(memory_space=pltpu.SMEM)] * 2 + [whole()] * (2 + len(queries)),
        out_specs=whole(),
        out_shape=jax.ShapeDtypeStruct((rows, width), jnp.bfloat16),
        compiler_params=pltpu.CompilerParams(vmem_limit_bytes=24 * MIB),
        cost_estimate=pl.CostEstimate(flops=1, bytes_accessed=1, transcendentals=0),
        name="attend",
    )(which, lengths, text, visual, *queries)


def line_gather(piece, axis):
    return jnp.concatenate(
        [piece, shift(piece, axis, 1), shift(piece, axis, -1), shift(piece, axis, 2)], axis=0
    )


def piece_table():
    turn = (0, -1, 1, 2)
    lines = [(0, 0), (0, -1), (0, 1), (1, 0), (0, 2), (1, -1), (1, 1), (1, 2)]
    ring_b = [(dz, by, t) for dz, by in lines for t in turn]
    ring_c = [(dz, t, by) for dz, by in lines for t in turn]
    return np.array(ring_b + ring_c, np.int32).T


def on_device(
    tokens,
    norm_gain,
    query_weight,
    query_bias,
    keyval_weight,
    keyval_bias,
    visual_keyval,
    caption_image,
    caption_length,
    image_owner,
):
    zl, x, y = (lax.axis_index(a) for a in DP)
    here = lax.axis_index(DP)
    rows = tokens.shape[0]
    depth = query_weight.shape[0]
    head_dim = keyval_weight.shape[2] // 2
    bias = jnp.concatenate([query_bias, keyval_bias.reshape(-1)]).astype(jnp.float32)[None]
    split = 3 * UNIT
    w_c = jnp.concatenate([keyval_weight.reshape(depth, -1), query_weight[:, :split]], axis=1)
    w_b = query_weight[:, split:]
    dz, dx, dy = piece_table()
    index = (zl + dz) % 2 * 16 + (x + dx) % 4 * 4 + (y + dy) % 4
    at_c = index.shape[0] // 2

    line_b = line_gather(w_b, "y")
    line_c = line_gather(w_c, "x")

    b_before, b_after = shift(line_b, "x", 1), shift(line_b, "x", -1)
    cross_b = shift(line_b, "zl", 1)
    c_before, c_after = shift(line_c, "y", 1), shift(line_c, "y", -1)

    tok_local = visual_keyval.shape[1]
    kv_heads = visual_keyval.shape[2]
    half = head_dim // 2
    length = rows // caption_image.shape[0]
    freqs = ROPE_BASE ** (-np.arange(half, dtype=np.float64) / half)
    angles = (tok_local * kv_heads + np.arange(length))[:, None] * freqs[None, :]
    angles = np.tile(angles, (TILE // length, 1))
    cos = np.concatenate([np.cos(angles)] * 2, axis=1).astype(np.float32)
    sin = np.concatenate([-np.sin(angles), np.sin(angles)], axis=1).astype(np.float32)
    tail = (bias, cos, sin)

    normed, normed_late = norm_rows(tokens, after(norm_gain, line_b, line_c), index, 7 * EACH)
    b_before, b_after, cross_b, c_before, c_after, z_line_c = (
        after(v, normed) for v in (b_before, b_after, cross_b, c_before, c_after, line_c)
    )
    cross_c = shift(z_line_c, "zl", 1)
    b_far, c_far = shift(b_before, "x", 1), shift(c_before, "y", 1)
    cb_before, cb_after = shift(cross_b, "x", 1), shift(cross_b, "x", -1)
    acc_b = project(normed, index, 0, [line_b, b_before, b_after])
    acc_c = project(normed, index, at_c, [line_c, c_before, c_after])

    images = image_owner.shape[0]
    chunk = tok_local // images
    own_visual = after(visual_keyval, acc_b, acc_c)
    spread = own_visual.reshape(images, chunk, kv_heads, 2 * head_dim).transpose(0, 2, 1, 3)
    spread = spread.reshape(images * kv_heads, chunk, 2 * head_dim)
    held = lax.all_to_all(spread, DP + MP, split_axis=0, concat_axis=0, tiled=True)

    b_far, c_far, cross_c, cb_before, cb_after = (
        after(v, spread) for v in (b_far, c_far, cross_c, cb_before, cb_after)
    )
    cc_before, cc_after = shift(cross_c, "y", 1), shift(cross_c, "y", -1)
    cc_far = shift(c_far, "zl", 1)
    cb_far = shift(cb_after, "x", -1)

    held = after(held, cross_c, c_far, cb_after)
    held = held.reshape(images, kv_heads * chunk, 2 * head_dim)
    wanted = jnp.stack([jnp.concatenate([image_owner[:1], image_owner[:-1]]), image_owner], axis=1)
    target = jnp.arange(images, dtype=jnp.int32)
    selector = (wanted[:, :, None] == target[None, None, :]).astype(jnp.bfloat16)
    sent = jnp.einsum(
        "isn,ntd->istd", selector, held, preferred_element_type=jnp.float32
    ).astype(jnp.bfloat16)
    visual = lax.all_to_all(sent, DP, split_axis=0, concat_axis=0, tiled=True)
    which = jnp.clip(caption_image - here + 1, 0, 1).astype(jnp.int32)

    cross_b, cross_c = after(cross_b, sent), after(cross_c, sent)
    acc_b = project(normed, index, 3 * EACH, [cross_b, b_far, cb_before, cb_after], acc_b)
    acc_c = project(normed, index, at_c + 3 * EACH, [cross_c, c_far], acc_c)
    cc_before, cc_after, cc_far = (after(v, acc_b, acc_c) for v in (cc_before, cc_after, cc_far))
    heads_c = project(
        normed, index, at_c + 5 * EACH, [cc_before, cc_after, cc_far], acc_c, SET_C, tail
    )
    cb_far = after(cb_far, heads_c)
    heads_b = project(normed_late, index, None, [cb_far], acc_b, SET_B, tail)
    visual = after(visual, heads_b)
    return attend(which, caption_length, heads_c, visual, [heads_c, heads_b], (2, 0))


def solution(mesh):
    grid = Mesh(mesh.devices.reshape(tuple(SIZES[a] for a in MESH_AXES)), MESH_AXES)
    placed = (
        P(DP, None),
        P(),
        P(DP, MP),
        P(MP),
        P(DP, MP, None),
        P(MP, None),
        P(DP, MP, None, None),
        P(DP),
        P(DP),
        P(),
    )
    return jax.shard_map(
        on_device, mesh=grid, in_specs=placed, out_specs=P(DP, MP), check_vma=False
    )
```
